32 devices in a mesh: dp: 8 (over z, core), mp: 4 (over y, x).
Axes of the slice: x: 2, y: 2, z: 4, core: 2. Of those that a mesh axis runs over, the one named last changes fastest.
Arguments:
- tokens: bfloat16 [16384, 768], P(('dp', 'mp')), may hold values from -6 to 6
- segments: int32 [32, 512], P(('dp', 'mp')), may hold values from 0 to 3, never falling along the last dimension, each value on 1 to 256 neighbouring positions
- routes: int32 [2, 16384, 1], P(None, ('dp', 'mp')), may hold values from 0 to 7; in each aligned block of 512 rows (0 to 511, 512 to 1023, ..., all dimensions but the last counted through in order) at most 72 rows name the same one
- gain_attn: float32 [2, 768], replicated, may hold values from 0.5 to 1.5
- qkv_weight: bfloat16 [2, 768, 2304], replicated, may hold values from -0.21875 to 0.21875
- out_weight: bfloat16 [2, 768, 768], replicated, may hold values from -2.5 to 2.5
- rel_bias: float32 [2, 32, 12], replicated, may hold values from -4 to 4
- gain_ffn: float32 [2, 768], replicated, may hold values from 0.5 to 1.5
- router_weight: float32 [2, 768, 8], replicated, may hold values from -0.109375 to 0.109375
- w_in: bfloat16 [2, 8, 768, 3072], P(None, 'dp', None, 'mp'), may hold values from -0.21875 to 0.21875
- w_out: bfloat16 [2, 8, 3072, 768], P(None, 'dp', 'mp'), may hold values from -1.25 to 1.25
- cotangent: bfloat16 [16384, 768], P(('dp', 'mp')), may hold values from -6 to 6
Outputs:
- output: float32 [16384, 768], P(('dp', 'mp'))
- grad_tokens: float32 [16384, 768], P(('dp', 'mp'))
- grad_gain_attn: float32 [2, 768], replicated
- grad_qkv: float32 [2, 768, 2304], replicated
- grad_out_weight: float32 [2, 768, 768], replicated
- grad_rel_bias: float32 [2, 32, 12], replicated
- grad_gain_ffn: float32 [2, 768], replicated
- grad_router: float32 [2, 768, 8], replicated
- grad_w_in: float32 [2, 8, 768, 3072], P(None, 'dp', None, 'mp')
- grad_w_out: float32 [2, 8, 3072, 768], P(None, 'dp', 'mp')
The draws below stay inside these ranges and needn't reach their ends.
Inputs may be any that keep to these rules, and one draw needn't show every extreme that they name: `routes`: in every layer the 512 rows of one device name no expert more than 72 times, and some device's rows name some expert exactly 72 times. `segments`: along each pack segment numbers never fall; a segment holds at most half of the 512 positions.
All inputs are finite; a program needn't handle non-finite values.
Results may differ from the reference program's by a relative error of at most 0.02.
Values may be sent and summed in bfloat16 or wider, within the bound.
No kernel may reach another device: no remote copies, remote signals or barrier semaphores. Data moves between devices by JAX's collectives and lax.ppermute only.
A program may use at most 320 MiB of HBM per device.

```python
import math
import jax
import jax.numpy as jnp
import numpy as np
from jax import lax

D = 768
HEADS = 12
HEAD_DIM = 64
FF = 3072
BUCKETS = 32
MAX_DIST = 128
LAYERS = 2
LEN = 512
EXPERTS = 8
TOK_DEV = 512
PACKS = 32
TOKENS = 16384
CAP = 72
DEVICES = 32


def shard_levels(stream_key, dims, cuts, smallest, largest):
    level = 1.0
    for dim, parts in cuts:
        steps = jax.random.uniform(jax.random.fold_in(jax.random.fold_in(stream_key, 6), dim), (parts,), jnp.float32, smallest / len(cuts), largest / len(cuts))
        level = level * jnp.repeat(jnp.exp(steps), dims[dim] // parts).reshape((-1,) + (1,) * (len(dims) - 1 - dim))
    return level


def split_up(count, total, limit, skew):
    portions = [(1 << 20) // math.isqrt(grade ** skew) + 1 for grade in range(2, count + 1)]
    rest, counts = total - limit - (count - 1), [1] * (count - 1)
    while rest > 0:
        candidates = [i for i in range(count - 1) if counts[i] < limit]
        mass, budget = sum([portions[i] for i in candidates]), rest
        for i in candidates:
            more = min(limit - counts[i], max(1, budget * portions[i] // mass), rest)
            counts[i] = counts[i] + more
            rest = rest - more
    return np.array([limit] + counts)


def uneven(rng, amount, total, limit, skew):
    if amount == 2:
        one = jax.random.randint(rng, (), max(1, total - limit), min(limit, total - 1) + 1)
        return jnp.stack([one, total - one])
    sizes = jnp.asarray(split_up(amount, total, limit, skew), jnp.int32)
    twos = (amount - 1) // 2
    source_of, taker = sizes[1:1 + 2 * twos:2], sizes[2:2 + 2 * twos:2]
    margin = jnp.minimum(source_of - 1, limit - taker)
    passed = jax.random.randint(jax.random.fold_in(rng, 1), (twos,), 0, 1 << 20) % (margin + 1)
    sizes = sizes.at[1:1 + 2 * twos:2].set(source_of - passed).at[2:2 + 2 * twos:2].set(taker + passed)
    return sizes[jax.random.permutation(jax.random.fold_in(rng, 2), amount)]


def routed_block(stream_key, own, number, rows, number_of, top, bound, lean):
    ranking = jax.random.permutation(stream_key, number_of)
    crowded, ordinary = load_shares(number_of, rows * top, bound, lean, True), load_shares(number_of, rows * top, bound, lean, False)
    places = jnp.arange(number_of)

    def named(sizes, rotation):
        used = int((sizes > 0).sum())
        fixed = max(1, used // 4)
        passed = fixed + (places - fixed + rotation * (used - fixed)) % max(1, number_of - fixed)
        return jnp.zeros((number_of,), jnp.int32).at[ranking[jnp.where(places < fixed, places, passed)]].set(jnp.asarray(sizes, jnp.int32))

    sizes = jnp.where(number % 4 == 0, named(crowded, number // 4), named(ordinary, number - number // 4 - 1))
    mixed = jax.random.permutation(jax.random.fold_in(own, 3), number_of)
    source_of, receiver = mixed[0:number_of // 2 * 2:2], mixed[1:number_of // 2 * 2:2]
    slack = jnp.minimum(sizes[source_of] - 1, bound - sizes[receiver]) // 2
    slack = jnp.where((source_of == ranking[0]) | (receiver == ranking[0]) | (sizes[receiver] == 0), 0, jnp.maximum(slack, 0))
    passed = jax.random.randint(jax.random.fold_in(own, 4), (number_of // 2,), 0, 1 << 20) % (slack + 1)
    sizes = sizes.at[source_of].add(-passed).at[receiver].add(passed)
    items = jnp.searchsorted(jnp.cumsum(sizes), jnp.arange(rows * top), side="right").astype(jnp.int32)
    grid = items.reshape(top, rows).T
    grid = grid[jax.random.permutation(jax.random.fold_in(own, 1), rows)]
    rotation = jax.random.randint(jax.random.fold_in(own, 2), (rows, 1), 0, top)
    return jnp.take_along_axis(grid, (jnp.arange(top)[None, :] + rotation) % top, axis=1)


def load_shares(number_of, total, most, slope, full):
    portions = [(1 << 20) // math.isqrt(rank ** slope) + 1 for rank in range(1, number_of + 1)]
    largest = most if full else min(most, max(-(-total // number_of), total * portions[0] // sum(portions)))
    least = 1 if total - largest >= number_of - 1 else 0
    holding, spare = [largest] + [least] * (number_of - 1), total - largest - least * (number_of - 1)
    while spare > 0:
        movable = [i for i in range(1, number_of) if holding[i] < largest] or [i for i in range(1, number_of) if holding[i] < most]
        mass, budget = sum([portions[i] for i in movable]), spare
        for i in movable:
            extra = min(most - holding[i], max(1, budget * portions[i] // mass), spare)
            holding[i] = holding[i] + extra
            spare = spare - extra
    return np.array(holding)


def centred(rng, extent, width, reach, split=(), kind=jnp.bfloat16):
    level = shard_levels(rng, extent, split, -0.22, 0.18) if split else 1.0
    drawn = jax.random.normal(rng, extent, jnp.float32) * width * level
    return jnp.minimum(jnp.maximum(drawn, -reach), reach).astype(kind)


def setup_inputs(seed: int = 0) -> dict:
    arg_keys = jax.random.split(jax.random.key(seed), 13)
    tokens = centred(arg_keys[0], (TOKENS, D), 1.0, 6.0, ((0, 32),))
    segments = jax.vmap(lambda own: jnp.searchsorted(jnp.cumsum(uneven(own, 4, LEN, LEN // 2, 2)), jnp.arange(LEN), side="right"))(jax.random.split(arg_keys[1], PACKS)).reshape((PACKS, LEN)).astype(jnp.int32)
    routes_keys = jax.random.split(jax.random.fold_in(arg_keys[2], 1), LAYERS * TOKENS // TOK_DEV)
    routes_turns = jax.random.permutation(jax.random.fold_in(arg_keys[2], 3), LAYERS * TOKENS // TOK_DEV)
    routes = jax.vmap(lambda own, number: routed_block(jax.random.fold_in(arg_keys[2], 2), own, number, TOK_DEV, EXPERTS, 1, CAP, 2))(routes_keys, routes_turns).reshape((LAYERS, TOKENS, 1))
    gain_attn = jnp.clip(1.0 + 0.1 * jax.random.normal(arg_keys[3], (LAYERS, D), jnp.float32), 0.5, 1.5)
    qkv_weight = centred(arg_keys[4], (LAYERS, D, 3 * D), D ** -0.5, 0.21875)
    out_weight = centred(arg_keys[5], (LAYERS, D, D), (max(D // 128, 1)) ** -0.5, 2.5)
    rel_bias = centred(arg_keys[6], (LAYERS, BUCKETS, HEADS), 1.0, 4.0, (), jnp.float32)
    gain_ffn = jnp.clip(1.0 + 0.1 * jax.random.normal(arg_keys[7], (LAYERS, D), jnp.float32), 0.5, 1.5)
    router_weight = centred(arg_keys[8], (LAYERS, D, EXPERTS), (4 * D) ** -0.5, 0.109375, (), jnp.float32)
    w_in = centred(arg_keys[9], (LAYERS, EXPERTS, D, FF), D ** -0.5, 0.21875, ((1, 8), (3, 4)))
    w_out = centred(arg_keys[10], (LAYERS, EXPERTS, FF, D), (max(FF // (2 * EXPERTS * EXPERTS), 1)) ** -0.5, 1.25, ((1, 8), (2, 4)))
    cotangent = centred(arg_keys[11], (TOKENS, D), 1.0, 6.0, ((0, 32),))
    return {"tokens": tokens, "segments": segments, "routes": routes, "gain_attn": gain_attn, "qkv_weight": qkv_weight, "out_weight": out_weight, "rel_bias": rel_bias, "gain_ffn": gain_ffn, "router_weight": router_weight, "w_in": w_in, "w_out": w_out, "cotangent": cotangent}


epsilon = 1e-06
masked_score = -1000000000.0
highest = lax.Precision.HIGHEST

@jax.custom_vjp
def low(v):
    return lax.optimization_barrier(v.astype(jnp.bfloat16)).astype(jnp.float32)

@jax.custom_vjp
def low_back(v):
    return v

def low_keep(v):
    return (low(v), None)

def low_pass(kept, grad):
    return (grad,)

def back_keep(v):
    return (v, None)

def back_low(kept, grad):
    return (low(grad),)
low.defvjp(low_keep, low_pass)
low_back.defvjp(back_keep, back_low)

def bucket_limits():
    half_count = BUCKETS // 2
    exact_count = half_count // 2
    lengths = np.arange(exact_count, 4 * MAX_DIST + 2 * LEN + 2)
    levels = (np.log(lengths / exact_count) / np.log(MAX_DIST / exact_count) * (half_count - exact_count)).astype(np.int64)
    levels = np.minimum(levels, half_count - exact_count - 1)
    limits = []
    for target in range(1, half_count - exact_count):
        limits.append(int(lengths[np.argmax(levels >= target)]))
    return limits

def bucket_of(distance):
    half_count = BUCKETS // 2
    exact_count = half_count // 2
    magnitude = jnp.abs(distance)
    counted = jnp.full(distance.shape, exact_count, jnp.int32)
    for limit_value in bucket_limits():
        counted = counted + (magnitude >= limit_value).astype(jnp.int32)
    return jnp.where(distance > 0, half_count, 0) + jnp.where(magnitude < exact_count, magnitude, counted)

def distance_onehot():
    distance = jnp.arange(-(LEN - 1), LEN, dtype=jnp.int32)
    buckets = bucket_of(distance)
    return (buckets[:, None] == jnp.arange(BUCKETS, dtype=jnp.int32)[None, :]).astype(jnp.float32)

def rms_apply(values, gain):
    factor = lax.rsqrt(lax.optimization_barrier(jnp.mean(values * values, axis=-1, keepdims=True)) + epsilon)
    return values * factor * gain

def router_gates(normed, weights, onehot):
    logits = jnp.dot(normed, weights, precision=highest)
    shifted = logits - lax.optimization_barrier(jnp.max(logits, axis=-1, keepdims=True))
    powers = jnp.exp(shifted)
    probability = powers / lax.optimization_barrier(jnp.sum(powers, axis=-1, keepdims=True))
    return lax.optimization_barrier(jnp.sum(probability * onehot, axis=-1))

def attend_pack(packed, qkv_w, out_w, bias_full):
    normed_pack, seg_pack = packed
    projected = low(low_back(jnp.dot(normed_pack, qkv_w, precision=highest)))
    heads_view = projected.reshape(LEN, 3, HEADS, HEAD_DIM)
    queries = heads_view[:, 0]
    key_heads = heads_view[:, 1]
    value_heads = heads_view[:, 2]
    scores = jnp.einsum('ihd,jhd->hij', queries, key_heads, precision=highest) * HEAD_DIM ** (-0.5) + bias_full
    same_segment = seg_pack[:, None] == seg_pack[None, :]
    scores = low_back(jnp.where(same_segment[None], scores, masked_score))
    row_max = lax.optimization_barrier(jnp.max(scores, axis=-1, keepdims=True))
    powers = jnp.exp(scores - row_max)
    probability = low(powers / lax.optimization_barrier(jnp.sum(powers, axis=-1, keepdims=True)))
    mixed = jnp.einsum('hij,jhd->ihd', probability, value_heads, precision=highest).reshape(LEN, HEADS * HEAD_DIM)
    mixed = low(low_back(mixed))
    return low_back(jnp.dot(mixed, out_w, precision=highest))

def experts_apply(normed, route_col, router_w, w_in_layer, w_out_layer):
    chosen = route_col[:, 0]
    expert_ids = jnp.arange(EXPERTS, dtype=jnp.int32)
    onehot_int = (chosen[:, None] == expert_ids[None, :]).astype(jnp.int32)
    onehot_float = onehot_int.astype(jnp.float32)
    gate_values = router_gates(normed, router_w, onehot_float)
    blocked = onehot_int.reshape(DEVICES, TOK_DEV, EXPERTS)
    slot_index = (lax.optimization_barrier(jnp.sum(jnp.cumsum(blocked, axis=1) * blocked, axis=-1)) - 1).reshape(TOKENS).astype(jnp.int32)
    owners = (jnp.arange(TOKENS, dtype=jnp.int32) // TOK_DEV).astype(jnp.int32)
    sent = low_back(normed)
    buffer = jnp.zeros((EXPERTS, DEVICES, CAP, D), jnp.float32).at[chosen, owners, slot_index].set(sent)

    def expert_rows(packed):
        rows_in, first_weight, second_weight = packed
        hidden = low_back(jnp.dot(rows_in, first_weight, precision=highest))
        active = low(jax.nn.gelu(hidden))
        return jnp.dot(active, second_weight, precision=highest)
    results = lax.map(jax.checkpoint(expert_rows), (buffer.reshape(EXPERTS, DEVICES * CAP, D), w_in_layer, w_out_layer))
    results = low(low_back(results)).reshape(EXPERTS, DEVICES, CAP, D)
    return gate_values[:, None] * results[chosen, owners, slot_index]

def layer_apply(values, segments, route_col, gain_one, qkv_w, out_w, rel_layer, gain_two, router_w, w_in_layer, w_out_layer):
    normed = low(rms_apply(values, gain_one))
    table = jnp.dot(distance_onehot(), rel_layer, precision=highest)
    offsets = jnp.arange(LEN, dtype=jnp.int32)
    position = offsets[None, :] - offsets[:, None] + (LEN - 1)
    bias_full = jnp.transpose(table[position], (2, 0, 1))

    def pack_apply(packed):
        return attend_pack(packed, qkv_w, out_w, bias_full)
    attended = lax.map(jax.checkpoint(pack_apply), (normed.reshape(PACKS, LEN, D), segments))
    middle = values + attended.reshape(TOKENS, D)
    normed_two = low(rms_apply(middle, gain_two))
    return middle + experts_apply(normed_two, route_col, router_w, w_in_layer, w_out_layer)

def reference(tokens, segments, routes, gain_attn, qkv_weight, out_weight, rel_bias, gain_ffn, router_weight, w_in, w_out, cotangent):

    def forward(values, gains_one, qkv_all, out_all, rel_all, gains_two, router_all, w_in_all, w_out_all):
        for layer_index in range(LAYERS):
            values = layer_apply(values, segments, routes[layer_index], gains_one[layer_index], qkv_all[layer_index], out_all[layer_index], rel_all[layer_index], gains_two[layer_index], router_all[layer_index], w_in_all[layer_index], w_out_all[layer_index])
        return values
    output, pullback = jax.vjp(forward, tokens.astype(jnp.float32), gain_attn.astype(jnp.float32), qkv_weight.astype(jnp.float32), out_weight.astype(jnp.float32), rel_bias.astype(jnp.float32), gain_ffn.astype(jnp.float32), router_weight.astype(jnp.float32), w_in.astype(jnp.float32), w_out.astype(jnp.float32))
    grads = pullback(cotangent.astype(jnp.float32))
    return (output, grads[0], grads[1], grads[2], grads[3], grads[4], grads[5], grads[6], grads[7], grads[8])
```

```python
import functools

import jax
import jax.numpy as jnp
import numpy as np
from jax import lax
from jax.experimental import pallas as pl
from jax.experimental.pallas import tpu as pltpu
from jax.sharding import PartitionSpec as P

HEAD_DIM = 64
BUCKETS = 32
MAX_DIST = 128
LAYERS = 2
LEN = 512

SIDE = 128
SPAN = 256
WINDOW_ROWS = 8
GROUP_HEADS = 4
GROUP = GROUP_HEADS * HEAD_DIM
PAIR = 2 * HEAD_DIM
VMEM_BYTES = 56 * 1024 * 1024

epsilon = 1e-06
masked_score = -1000000000.0
highest = lax.Precision.HIGHEST
f32 = jnp.float32
bf16 = jnp.bfloat16

NT = (((1,), (1,)), ((), ()))
TN = (((0,), (0,)), ((), ()))


def bucket_limits():
    half_count = BUCKETS // 2
    exact_count = half_count // 2
    lengths = np.arange(exact_count, 4 * MAX_DIST + 2 * LEN + 2)
    levels = (
        np.log(lengths / exact_count) / np.log(MAX_DIST / exact_count) * (half_count - exact_count)
    ).astype(np.int64)
    levels = np.minimum(levels, half_count - exact_count - 1)
    limits = []
    for target in range(1, half_count - exact_count):
        limits.append(int(lengths[np.argmax(levels >= target)]))
    return limits


def bucket_of(distance):
    half_count = BUCKETS // 2
    exact_count = half_count // 2
    magnitude = np.abs(distance)
    counted = np.full(distance.shape, exact_count, np.int32)
    for limit_value in bucket_limits():
        counted = counted + (magnitude >= limit_value).astype(np.int32)
    return np.where(distance > 0, half_count, 0) + np.where(
        magnitude < exact_count, magnitude, counted
    )


def window_buckets():
    place = np.arange(SPAN)
    shift = np.where(place < SIDE, -place, SPAN - place)
    rows = [bucket_of(offset * SIDE + shift) for offset in (-1, 0, 1)]
    for row in rows:
        row[SIDE] = -1
    far = bucket_of(np.array([-2 * SIDE + SIDE - 1, 2 * SIDE - SIDE + 1]))
    rows += [np.full(SPAN, far[0]), np.full(SPAN, far[1])]
    rows += [np.full(SPAN, -1)] * (WINDOW_ROWS - len(rows))
    return np.stack(rows).astype(np.int32)


def window_onehot():
    return (
        jnp.asarray(window_buckets().reshape(-1))[:, None]
        == jnp.arange(BUCKETS, dtype=jnp.int32)[None, :]
    ).astype(f32)


def params(**extra):
    return pltpu.CompilerParams(vmem_limit_bytes=VMEM_BYTES, **extra)


def dot(a, b, dims=None, precision=None):
    if dims is None:
        return jnp.dot(a, b, preferred_element_type=f32, precision=precision)
    return lax.dot_general(a, b, dims, preferred_element_type=f32, precision=precision)


def rms_factor(values):
    return lax.rsqrt(jnp.mean(values * values, axis=-1, keepdims=True) + epsilon)


def half_mask(half):
    lane = lax.broadcasted_iota(jnp.int32, (1, PAIR), 1)
    inside = (lane >= half * HEAD_DIM) & (lane < (half + 1) * HEAD_DIM)
    return inside.astype(f32)


def bias_blocks(windows):
    blocks = {}
    for row, offset in enumerate((-1, 0, 1)):
        spread = jnp.broadcast_to(windows[row : row + 1, :], (SIDE, SPAN))
        blocks[offset] = pltpu.roll(spread, 0, 1, stride=1, stride_axis=0)[:, :SIDE]
    blocks[-2] = jnp.broadcast_to(windows[3:4, :SIDE], (SIDE, SIDE))
    blocks[2] = jnp.broadcast_to(windows[4:5, :SIDE], (SIDE, SIDE))
    return blocks


def offset_of(key_block, query_block):
    return max(-2, min(2, key_block - query_block))


def bias_part(blocks, first_query, width):
    columns = []
    for query_block in range(first_query // SIDE, (first_query + width) // SIDE):
        columns.append(
            jnp.concatenate(
                [blocks[offset_of(key_block, query_block)] for key_block in range(LEN // SIDE)],
                axis=0,
            )
        )
    return jnp.concatenate(columns, axis=1)


def diagonal_sums(block):
    padded = jnp.concatenate([block, jnp.zeros((SIDE, SPAN - SIDE), f32)], axis=1)
    total = padded[:8]
    for first in range(8, SIDE, 8):
        total = total + pltpu.roll(padded[first : first + 8], SPAN - first, 1)
    row = lax.broadcasted_iota(jnp.int32, (8, SPAN), 0)
    for bit in (1, 2, 4):
        total = jnp.where((row & bit) != 0, pltpu.roll(total, SPAN - bit, 1), total)
    return jnp.sum(total, axis=0, keepdims=True)


def mask_of(seg_col, seg_row):
    return jnp.where(seg_col == seg_row, 0.0, masked_score).astype(f32)


def place_matrix(rowid_row, count):
    rows = lax.broadcasted_iota(jnp.int32, (count, rowid_row.shape[1]), 0)
    return (rows == rowid_row).astype(bf16)


def take_matrix(rowid_col, count):
    lanes = lax.broadcasted_iota(jnp.int32, (rowid_col.shape[0], count), 1)
    return (lanes == rowid_col).astype(bf16)


def route_onehot(route_col, experts):
    lanes = lax.broadcasted_iota(jnp.int32, (route_col.shape[0], experts), 1)
    return (lanes == route_col).astype(f32)


QUERY_SPAN = 256


def attend_kernel(combine, refs):
    refs = list(refs)
    take = lambda count: [refs.pop(0) for _ in range(count)]
    if combine:
        middle_prev, prob_prev, back_prev, rowcol_prev, route_prev = take(5)
    else:
        (tokens,) = take(1)
    gain_attn, wq, wk, wv, wout, windows, seg_row, seg_col = take(8)
    gain_ffn, router, rowid_row = take(3)
    if combine:
        (x_out,) = take(1)
    proj, mixed, lse, middle, prob, buffer = take(6)
    normed_s, x_s, acc_s, mask_s = take(4)
    step = pl.program_id(0)

    @pl.when(step == 0)
    def _():
        if combine:
            chosen = route_onehot(route_prev[...], prob_prev.shape[1])
            gate = jnp.sum(prob_prev[...] * chosen, axis=-1, keepdims=True)
            returned = dot(take_matrix(rowcol_prev[...], back_prev.shape[0]), back_prev[...])
            x = middle_prev[...] + gate * returned
            x_out[...] = x
        else:
            x = tokens[...].astype(f32)
        x_s[...] = x
        normed_s[...] = (x * rms_factor(x) * gain_attn[...]).astype(bf16)
        acc_s[...] = jnp.zeros_like(acc_s)
        mask_s[...] = mask_of(seg_col[...], seg_row[...])

    normed = normed_s[...]
    q = dot(normed, wq[...]).astype(bf16)
    k = dot(normed, wk[...]).astype(bf16)
    v = dot(normed, wv[...]).astype(bf16)
    proj[0] = q
    proj[1] = k
    proj[2] = v
    for pair in range(GROUP_HEADS // 2):
        lanes = slice(pair * PAIR, (pair + 1) * PAIR)
        q2 = q[:, lanes].astype(f32) * HEAD_DIM ** (-0.5)
        k2 = k[:, lanes]
        v2t = v[:, lanes].T
        outs = []
        for half in range(2):
            head = pair * 2 + half
            qm = (q2 * half_mask(half)).astype(bf16)
            vt = v2t[half * HEAD_DIM : (half + 1) * HEAD_DIM, :]
            blocks = bias_blocks(windows[head])
            parts = []
            for first in range(0, LEN, QUERY_SPAN):
                span = slice(first, first + QUERY_SPAN)
                scores = dot(k2, qm[span], NT)
                scores = scores + bias_part(blocks, first, QUERY_SPAN) + mask_s[:, span]
                top = jnp.max(scores, axis=0, keepdims=True)
                powers = jnp.exp(scores - top)
                total = jnp.sum(powers, axis=0, keepdims=True)
                parts.append(dot(vt, powers.astype(bf16)) * (1.0 / total))
                lse[0, head : head + 1, span] = top + jnp.log(total)
            outs.append(jnp.concatenate(parts, axis=1))
        mixed[:, lanes] = jnp.concatenate(outs, axis=0).T.astype(bf16)
    acc_s[...] += dot(mixed[...], wout[...])

    @pl.when(step == pl.num_programs(0) - 1)
    def _():
        mid = x_s[...] + acc_s[...]
        middle[...] = mid
        nf = (mid * rms_factor(mid) * gain_ffn[...]).astype(bf16)
        logits = dot(nf.astype(f32), router[...], precision=highest)
        powers = jnp.exp(logits - jnp.max(logits, axis=-1, keepdims=True))
        prob[...] = powers / jnp.sum(powers, axis=-1, keepdims=True)
        buffer[...] = dot(place_matrix(rowid_row[...], buffer.shape[0]), nf).astype(bf16)


def whole(array):
    zeros = (0,) * array.ndim
    return pl.BlockSpec(array.shape, lambda g: zeros)


def whole_shape(shape):
    zeros = (0,) * len(shape)
    return pl.BlockSpec(shape, lambda g: zeros)


def qkv_specs(width):
    per = width // GROUP
    return [
        pl.BlockSpec((width, GROUP), functools.partial(lambda part, g: (0, part * per + g), part))
        for part in range(3)
    ]


def attend(source, gain_attn, qkv_w, out_w, windows, seg_row, seg_col, gain_ffn, router, rowid_row):
    combine = len(source) > 1
    width = qkv_w.shape[0]
    groups = width // GROUP
    experts = router.shape[1]
    count = rowid_row.rows
    ins = list(source) + [gain_attn, qkv_w, qkv_w, qkv_w, out_w, windows, seg_row, seg_col]
    ins += [gain_ffn, router, rowid_row.array]
    specs = [whole(a) for a in source] + [whole(gain_attn)] + qkv_specs(width)
    specs += [pl.BlockSpec((GROUP, width), lambda g: (g, 0))]
    specs += [pl.BlockSpec((GROUP_HEADS, WINDOW_ROWS, SPAN), lambda g: (g, 0, 0))]
    specs += [whole(seg_row), whole(seg_col), whole(gain_ffn), whole(router), whole(rowid_row.array)]
    shapes = [
        ((3, LEN, width), bf16, pl.BlockSpec((3, LEN, GROUP), lambda g: (0, 0, g))),
        ((LEN, width), bf16, pl.BlockSpec((LEN, GROUP), lambda g: (0, g))),
        ((groups, 8, LEN), f32, pl.BlockSpec((1, 8, LEN), lambda g: (g, 0, 0))),
        ((LEN, width), f32, whole_shape((LEN, width))),
        ((LEN, experts), f32, whole_shape((LEN, experts))),
        ((count, width), bf16, whole_shape((count, width))),
    ]
    if combine:
        shapes = [((LEN, width), f32, whole_shape((LEN, width)))] + shapes
    return pl.pallas_call(
        lambda *refs: attend_kernel(combine, refs),
        grid=(groups,),
        in_specs=specs,
        out_specs=[s[2] for s in shapes],
        out_shape=[jax.ShapeDtypeStruct(s[0], s[1]) for s in shapes],
        scratch_shapes=[
            pltpu.VMEM((LEN, width), bf16),
            pltpu.VMEM((LEN, width), f32),
            pltpu.VMEM((LEN, width), f32),
            pltpu.VMEM((LEN, LEN), f32),
        ],
        compiler_params=params(),
        cost_estimate=pl.CostEstimate(
            flops=8 * LEN * width * width + 4 * LEN * LEN * width,
            bytes_accessed=16 * LEN * width + 8 * width * width,
            transcendentals=LEN * LEN * width // HEAD_DIM,
        ),
        name="attend",
    )(*ins)


def attend_back_kernel(first_layer, refs):
    refs = list(refs)
    take = lambda count: [refs.pop(0) for _ in range(count)]
    gradient, gback, rowcol, gate_grad, prob, route_col, middle, gain_ffn, router = take(9)
    x_ref, gain_attn, wq, wk, wv, wout, proj, mixed, lse, windows, seg_row, seg_col = take(12)
    if not first_layer:
        back_prev, rowrow_prev, rowcol_prev, prob_prev, route_prev = take(5)
    grad_in, gq, gk, gv, gout, gwin, gain_attn_g, gain_ffn_g, grouter = take(9)
    if not first_layer:
        buffer_prev, gate_grad_prev = take(2)
    normt_s, mg_s, att_s, acc_s, mask_s = take(5)
    step = pl.program_id(0)

    @pl.when(step == 0)
    def _():
        g = gradient[...].astype(f32)
        expert_part = dot(take_matrix(rowcol[...], gback.shape[0]), gback[...])
        probability = prob[...]
        chosen = route_onehot(route_col[...], prob.shape[1])
        gate = jnp.sum(probability * chosen, axis=-1, keepdims=True)
        logit_grad = gate_grad[...] * gate * (chosen - probability)
        mid = middle[...]
        r = rms_factor(mid)
        scaled = mid * r
        nf = (scaled * gain_ffn[...]).astype(bf16).astype(f32)
        grouter[...] = dot(logit_grad, nf, TN, precision=highest)
        ffn_in = expert_part + dot(logit_grad, router[...], NT, precision=highest)
        u = ffn_in * gain_ffn[...]
        mg = g + r * (u - scaled * (r * jnp.mean(u * mid, axis=-1, keepdims=True)))
        gain_ffn_g[...] = jnp.sum(ffn_in * scaled, axis=0, keepdims=True)
        mg_s[...] = mg
        att_s[...] = mg.astype(bf16)
        x = x_ref[...].astype(f32)
        normed = (x * rms_factor(x) * gain_attn[...]).astype(bf16)
        normt_s[...] = normed.T
        acc_s[...] = jnp.zeros_like(acc_s)
        mask_s[...] = mask_of(seg_col[...], seg_row[...])

    att = att_s[...]
    gout[...] = dot(mixed[...], att, TN).astype(gout.dtype)
    mixed_grad = dot(att, wout[...], NT).astype(bf16)
    dqs, dks, dvs = [], [], []
    for pair in range(GROUP_HEADS // 2):
        lanes = slice(pair * PAIR, (pair + 1) * PAIR)
        q2 = proj[0, :, lanes].astype(f32) * HEAD_DIM ** (-0.5)
        k2 = proj[1, :, lanes]
        v2 = proj[2, :, lanes]
        k2t = k2.T
        o2 = mixed_grad[:, lanes].astype(f32)
        dk = jnp.zeros((LEN, PAIR), f32)
        dv = jnp.zeros((LEN, PAIR), f32)
        dqts = []
        for half in range(2):
            head = pair * 2 + half
            qm = (q2 * half_mask(half)).astype(bf16)
            om = (o2 * half_mask(half)).astype(bf16)
            kt = k2t[half * HEAD_DIM : (half + 1) * HEAD_DIM, :]
            blocks = bias_blocks(windows[head])
            sums = {}
            parts = []
            for first in range(0, LEN, QUERY_SPAN):
                span = slice(first, first + QUERY_SPAN)
                scores = dot(k2, qm[span], NT)
                scores = scores + bias_part(blocks, first, QUERY_SPAN) + mask_s[:, span]
                powers = jnp.exp(scores - lse[0, head : head + 1, span])
                prob_grad = dot(v2, om[span], NT)
                weighted = powers * prob_grad
                delta = jnp.sum(weighted, axis=0, keepdims=True)
                score_grad = weighted - powers * delta
                for kb in range(LEN // SIDE):
                    for qb in range(QUERY_SPAN // SIDE):
                        piece = score_grad[kb * SIDE : (kb + 1) * SIDE, qb * SIDE : (qb + 1) * SIDE]
                        offset = offset_of(kb, qb + first // SIDE)
                        sums[offset] = sums[offset] + piece if offset in sums else piece
                sg = score_grad.astype(bf16)
                dv = dv + dot(powers.astype(bf16), om[span])
                dk = dk + dot(sg, qm[span])
                parts.append(dot(kt, sg))
            dqts.append(jnp.concatenate(parts, axis=1))
            for row, offset in enumerate((-1, 0, 1)):
                gwin[head, row : row + 1, :] = diagonal_sums(sums[offset])
            for row, offset in ((3, -2), (4, 2)):
                gwin[head, row : row + 1, :SIDE] = jnp.sum(sums[offset], axis=0, keepdims=True)
                gwin[head, row : row + 1, SIDE:] = jnp.zeros((1, SPAN - SIDE), f32)
            gwin[head, 5:WINDOW_ROWS, :] = jnp.zeros((WINDOW_ROWS - 5, SPAN), f32)
        dqs.append((jnp.concatenate(dqts, axis=0) * HEAD_DIM ** (-0.5)).T)
        dks.append(dk)
        dvs.append(dv)
    total = acc_s[...]
    for ref, weight, pieces in ((gq, wq, dqs), (gk, wk, dks), (gv, wv, dvs)):
        part = jnp.concatenate(pieces, axis=1).astype(bf16)
        ref[...] = dot(normt_s[...], part).astype(ref.dtype)
        total = total + dot(part, weight[...], NT)
    acc_s[...] = total

    @pl.when(step == pl.num_programs(0) - 1)
    def _():
        x = x_ref[...].astype(f32)
        r = rms_factor(x)
        scaled = x * r
        attn_in = acc_s[...]
        u = attn_in * gain_attn[...]
        g = mg_s[...] + r * (u - scaled * (r * jnp.mean(u * x, axis=-1, keepdims=True)))
        gain_attn_g[...] = jnp.sum(attn_in * scaled, axis=0, keepdims=True)
        grad_in[...] = g
        if not first_layer:
            send_back(
                g, back_prev, rowrow_prev, rowcol_prev, prob_prev, route_prev, buffer_prev, gate_grad_prev
            )


def send_back(g, back, rowrow, rowcol, prob, route_col, buffer, gate_grad):
    returned = dot(take_matrix(rowcol[...], back.shape[0]), back[...])
    gate = jnp.sum(
        prob[...] * route_onehot(route_col[...], prob.shape[1]), axis=-1, keepdims=True
    )
    gate_grad[...] = jnp.sum(g * returned, axis=-1, keepdims=True)
    expert_grad = (gate * g).astype(bf16)
    buffer[...] = dot(place_matrix(rowrow[...], buffer.shape[0]), expert_grad).astype(bf16)
    return gate * returned


def attend_back(state, gradient, gback, gate_grad, previous, common):
    first_layer = previous is None
    width = common["out_w"].shape[0]
    groups = width // GROUP
    experts = common["router"].shape[1]
    ins, specs = [], []

    def add(array, spec=None):
        ins.append(array)
        specs.append(whole(array) if spec is None else spec)

    for array in (gradient, gback, state["rowcol"], gate_grad, state["prob"], state["route_col"]):
        add(array)
    for array in (state["middle"], common["gain_ffn"], common["router"], state["x"]):
        add(array)
    add(common["gain_attn"])
    for spec in qkv_specs(width):
        add(common["qkv_w"], spec)
    add(common["out_w"], pl.BlockSpec((GROUP, width), lambda g: (g, 0)))
    add(state["proj"], pl.BlockSpec((3, LEN, GROUP), lambda g: (0, 0, g)))
    add(state["mixed"], pl.BlockSpec((LEN, GROUP), lambda g: (0, g)))
    add(state["lse"], pl.BlockSpec((1, 8, LEN), lambda g: (g, 0, 0)))
    add(common["windows"], pl.BlockSpec((GROUP_HEADS, WINDOW_ROWS, SPAN), lambda g: (g, 0, 0)))
    add(common["seg_row"])
    add(common["seg_col"])
    if not first_layer:
        for name in ("back", "rowrow", "rowcol", "prob", "route_col"):
            add(previous[name])
    column = pl.BlockSpec((width, GROUP), lambda g: (0, g))
    shapes = [
        ((LEN, width), f32, whole_shape((LEN, width))),
        ((width, width), bf16, column),
        ((width, width), bf16, column),
        ((width, width), bf16, column),
        ((width, width), bf16, pl.BlockSpec((GROUP, width), lambda g: (g, 0))),
        (
            common["windows"].shape,
            f32,
            pl.BlockSpec((GROUP_HEADS, WINDOW_ROWS, SPAN), lambda g: (g, 0, 0)),
        ),
        ((1, width), f32, whole_shape((1, width))),
        ((1, width), f32, whole_shape((1, width))),
        ((experts, width), f32, whole_shape((experts, width))),
    ]
    if not first_layer:
        count = previous["back"].shape[0]
        shapes += [
            ((count, width), bf16, whole_shape((count, width))),
            ((LEN, 1), f32, whole_shape((LEN, 1))),
        ]
    return pl.pallas_call(
        lambda *refs: attend_back_kernel(first_layer, refs),
        grid=(groups,),
        in_specs=specs,
        out_specs=[s[2] for s in shapes],
        out_shape=[jax.ShapeDtypeStruct(s[0], s[1]) for s in shapes],
        scratch_shapes=[
            pltpu.VMEM((width, LEN), bf16),
            pltpu.VMEM((LEN, width), f32),
            pltpu.VMEM((LEN, width), bf16),
            pltpu.VMEM((LEN, width), f32),
            pltpu.VMEM((LEN, LEN), f32),
        ],
        compiler_params=params(),
        cost_estimate=pl.CostEstimate(
            flops=16 * LEN * width * width + 10 * LEN * LEN * width,
            bytes_accessed=30 * LEN * width + 16 * width * width,
            transcendentals=LEN * LEN * width // HEAD_DIM,
        ),
        name="attend_back",
    )(*ins)


def turn_kernel(middle, cotangent, back, rowrow, rowcol, prob, route_col, output, buffer, gate_grad):
    g = cotangent[...].astype(f32)
    added = send_back(g, back, rowrow, rowcol, prob, route_col, buffer, gate_grad)
    output[...] = middle[...] + added


def turn(state, cotangent):
    width = cotangent.shape[1]
    count = state["back"].shape[0]
    return pl.pallas_call(
        turn_kernel,
        out_shape=[
            jax.ShapeDtypeStruct((LEN, width), f32),
            jax.ShapeDtypeStruct((count, width), bf16),
            jax.ShapeDtypeStruct((LEN, 1), f32),
        ],
        compiler_params=params(),
        cost_estimate=pl.CostEstimate(
            flops=4 * LEN * count * width, bytes_accessed=14 * LEN * width, transcendentals=0
        ),
        name="turn",
    )(
        state["middle"],
        cotangent,
        state["back"],
        state["rowrow"],
        state["rowcol"],
        state["prob"],
        state["route_col"],
    )


GELU_A = float(np.sqrt(2.0 / np.pi))
GELU_B = 0.044715


def gelu_tanh(hidden):
    return jnp.tanh(GELU_A * (hidden + GELU_B * (hidden * hidden * hidden)))


def gelu_of(hidden, curve):
    return 0.5 * hidden * (1.0 + curve)


def gelu_slope(hidden, curve):
    inner = GELU_A * (1.0 + (3.0 * GELU_B) * (hidden * hidden))
    return 0.5 * (1.0 + curve) + 0.5 * hidden * (1.0 - curve * curve) * inner


def expert_kernel(rows, w_in, w_out, out, acc):
    step = pl.program_id(0)

    @pl.when(step == 0)
    def _():
        acc[...] = jnp.zeros_like(acc)

    hidden = dot(rows[...], w_in[0])
    active = gelu_of(hidden, gelu_tanh(hidden)).astype(bf16)
    acc[...] += dot(active, w_out[0])

    @pl.when(step == pl.num_programs(0) - 1)
    def _():
        out[...] = acc[...].astype(bf16)


def expert(rows, w_in_all, w_out_all):
    parts, width, part = w_in_all.shape
    count = rows.shape[0]
    return pl.pallas_call(
        expert_kernel,
        grid=(parts,),
        in_specs=[
            whole(rows),
            pl.BlockSpec((1, width, part), lambda b: (b, 0, 0)),
            pl.BlockSpec((1, part, width), lambda b: (b, 0, 0)),
        ],
        out_specs=whole(rows),
        out_shape=jax.ShapeDtypeStruct(rows.shape, bf16),
        scratch_shapes=[pltpu.VMEM(rows.shape, f32)],
        compiler_params=params(),
        cost_estimate=pl.CostEstimate(
            flops=4 * count * width * parts * part,
            bytes_accessed=4 * count * width + 4 * width * parts * part,
            transcendentals=count * parts * part,
        ),
        name="expert",
    )(rows, w_in_all, w_out_all)


def expert_back_kernel(rows, grads, w_in, w_out, out, acc):
    step = pl.program_id(0)

    @pl.when(step == 0)
    def _():
        acc[...] = jnp.zeros_like(acc)

    hidden = dot(rows[...], w_in[0])
    act_grad = dot(grads[...], w_out[0], NT)
    pre_grad = (act_grad * gelu_slope(hidden, gelu_tanh(hidden))).astype(bf16)
    acc[...] += dot(pre_grad, w_in[0], NT)

    @pl.when(step == pl.num_programs(0) - 1)
    def _():
        out[...] = acc[...].astype(bf16)


def expert_back(rows, grads, w_in_all, w_out_all):
    parts, width, part = w_in_all.shape
    count = rows.shape[0]
    return pl.pallas_call(
        expert_back_kernel,
        grid=(parts,),
        in_specs=[
            whole(rows),
            whole(grads),
            pl.BlockSpec((1, width, part), lambda b: (b, 0, 0)),
            pl.BlockSpec((1, part, width), lambda b: (b, 0, 0)),
        ],
        out_specs=whole(rows),
        out_shape=jax.ShapeDtypeStruct(rows.shape, bf16),
        scratch_shapes=[pltpu.VMEM(rows.shape, f32)],
        compiler_params=params(),
        cost_estimate=pl.CostEstimate(
            flops=6 * count * width * parts * part,
            bytes_accessed=6 * count * width + 4 * width * parts * part,
            transcendentals=count * parts * part,
        ),
        name="expert_back",
    )(rows, grads, w_in_all, w_out_all)


def weight_grad_kernel(rows, grads, w_in, w_out, g_in, g_out):
    step = pl.program_id(0)

    @pl.when(step == 0)
    def _():
        g_in[...] = jnp.zeros_like(g_in)
        g_out[...] = jnp.zeros_like(g_out)

    hidden = dot(rows[...], w_in[...])
    curve = gelu_tanh(hidden)
    active = gelu_of(hidden, curve).astype(bf16)
    act_grad = dot(grads[...], w_out[...], NT)
    pre_grad = (act_grad * gelu_slope(hidden, curve)).astype(bf16)
    g_out[...] += dot(active, grads[...], TN)
    g_in[...] += dot(rows[...], pre_grad, TN)


def weight_grad(rows_all, grads_all, w_in, w_out, parts):
    width, part = w_in.shape
    count = rows_all.shape[0] // parts
    block = pl.BlockSpec((count, width), lambda b: (b, 0))
    return pl.pallas_call(
        weight_grad_kernel,
        grid=(parts,),
        in_specs=[block, block, whole(w_in), whole(w_out)],
        out_specs=[whole(w_in), whole(w_out)],
        out_shape=[
            jax.ShapeDtypeStruct(w_in.shape, f32),
            jax.ShapeDtypeStruct(w_out.shape, f32),
        ],
        compiler_params=params(),
        cost_estimate=pl.CostEstimate(
            flops=8 * rows_all.shape[0] * width * part,
            bytes_accessed=4 * rows_all.shape[0] * width + 12 * width * part,
            transcendentals=rows_all.shape[0] * part,
        ),
        name="weight_grad",
    )(rows_all, grads_all, w_in, w_out)


class Places:
    def __init__(self, array, rows):
        self.array = array
        self.rows = rows


def swap(rows, experts):
    count, width = rows.shape
    split = rows.reshape(experts, count // experts, width)
    return lax.all_to_all(split, "dp", split_axis=0, concat_axis=0, tiled=True).reshape(count, width)


def gather_parts(array):
    return lax.all_gather(array, "mp", axis=0, tiled=True)


def body(
    tokens,
    segments,
    routes,
    gain_attn,
    qkv_weight,
    out_weight,
    rel_bias,
    gain_ffn,
    router_weight,
    w_in,
    w_out,
    cotangent,
):
    tok_count, width = tokens.shape
    experts = w_in.shape[1] * lax.axis_size("dp")
    parts = lax.axis_size("mp")
    capacity = (tok_count * 9 + 8 * experts - 1) // (8 * experts)
    count = experts * capacity
    heads = width // HEAD_DIM

    onehot = window_onehot()
    windows = [
        jnp.dot(onehot, rel_bias[layer], precision=highest).T.reshape(heads, WINDOW_ROWS, SPAN)
        for layer in range(LAYERS)
    ]
    chosen = routes[:, :, 0]
    chosen_onehot = (
        chosen[:, :, None] == jnp.arange(experts, dtype=jnp.int32)[None, None, :]
    ).astype(jnp.int32)
    slots = jnp.sum(jnp.cumsum(chosen_onehot, axis=1) * chosen_onehot, axis=-1) - 1
    rowid = chosen * capacity + slots
    seg_row = segments.reshape(1, LEN)
    seg_col = segments.reshape(LEN, 1)

    w_all = [(gather_parts(w_in[layer]), gather_parts(w_out[layer])) for layer in range(LAYERS)]
    states = []
    source = (tokens,)
    for layer in range(LAYERS):
        common = dict(
            gain_attn=gain_attn[layer : layer + 1],
            gain_ffn=gain_ffn[layer : layer + 1],
            qkv_w=qkv_weight[layer],
            out_w=out_weight[layer],
            router=router_weight[layer],
            windows=windows[layer],
            seg_row=seg_row,
            seg_col=seg_col,
        )
        state = dict(
            common=common,
            rowrow=rowid[layer].reshape(1, tok_count),
            rowcol=rowid[layer].reshape(tok_count, 1),
            route_col=routes[layer],
        )
        results = attend(
            source,
            common["gain_attn"],
            common["qkv_w"],
            common["out_w"],
            common["windows"],
            seg_row,
            seg_col,
            common["gain_ffn"],
            common["router"],
            Places(state["rowrow"], count),
        )
        if layer > 0:
            state["x"] = results[0]
            results = results[1:]
        else:
            state["x"] = tokens
        for name, value in zip(("proj", "mixed", "lse", "middle", "prob"), results):
            state[name] = value
        rows = swap(results[5], experts)
        state["rows"] = rows
        state["back"] = swap(expert(rows, *w_all[layer]), experts)
        states.append(state)
        source = tuple(state[name] for name in ("middle", "prob", "back", "rowcol", "route_col"))

    rows_all = [gather_parts(state["rows"]) for state in states]
    output, buffer, gate_grad = turn(states[-1], cotangent)
    gradient = cotangent
    per_layer = [None] * LAYERS
    for layer in reversed(range(LAYERS)):
        state = states[layer]
        grads = swap(buffer, experts)
        sent = expert_back(state["rows"], grads, *w_all[layer])
        gback = swap(sent, experts)
        grads_all = gather_parts(grads)
        g_in, g_out = weight_grad(rows_all[layer], grads_all, w_in[layer, 0], w_out[layer, 0], parts)
        previous = states[layer - 1] if layer > 0 else None
        results = attend_back(state, gradient, gback, gate_grad, previous, state["common"])
        gradient, gq, gk, gv, gout, gwin, gain_a, gain_f, grouter = results[:9]
        if layer > 0:
            buffer, gate_grad = results[9:]
        big = lax.psum((gq, gk, gv, gout), ("dp", "mp"))
        small = (
            gain_a,
            gain_f,
            grouter,
            jnp.dot(
                onehot.T, gwin.reshape(heads, WINDOW_ROWS * SPAN).T, precision=highest
            ),
        )
        per_layer[layer] = (big, small, g_in, g_out)
    small = lax.psum([entry[1] for entry in per_layer], ("dp", "mp"))
    grad_qkv = jnp.stack(
        [jnp.concatenate(entry[0][:3], axis=1).astype(f32) for entry in per_layer]
    )
    grad_out = jnp.stack([entry[0][3].astype(f32) for entry in per_layer])
    grad_gain_attn = jnp.concatenate([entry[0] for entry in small], axis=0)
    grad_gain_ffn = jnp.concatenate([entry[1] for entry in small], axis=0)
    grad_router = jnp.stack([entry[2].T for entry in small])
    grad_rel = jnp.stack([entry[3] for entry in small])
    grad_w_in = jnp.stack([entry[2] for entry in per_layer])[:, None]
    grad_w_out = jnp.stack([entry[3] for entry in per_layer])[:, None]
    return (
        output,
        gradient,
        grad_gain_attn,
        grad_qkv,
        grad_out,
        grad_rel,
        grad_gain_ffn,
        grad_router,
        grad_w_in,
        grad_w_out,
    )


def solution(mesh):
    return jax.shard_map(
        body,
        mesh=mesh,
        in_specs=(
            P(("dp", "mp"), None),
            P(("dp", "mp"), None),
            P(None, ("dp", "mp"), None),
            P(),
            P(),
            P(),
            P(),
            P(),
            P(),
            P(None, "dp", None, "mp"),
            P(None, "dp", "mp", None),
            P(("dp", "mp"), None),
        ),
        out_specs=(
            P(("dp", "mp"), None),
            P(("dp", "mp"), None),
            P(),
            P(),
            P(),
            P(),
            P(),
            P(),
            P(None, "dp", None, "mp"),
            P(None, "dp", "mp", None),
        ),
        check_vma=False,
    )
```

```python
import functools

import jax
import jax.numpy as jnp
import numpy as np
from jax import lax
from jax.experimental import pallas as pl
from jax.experimental.pallas import tpu as pltpu
from jax.sharding import PartitionSpec as P

HEAD_DIM = 64
BUCKETS = 32
MAX_DIST = 128
LAYERS = 2
LEN = 512

SIDE = 128
SPAN = 256
WINDOW_ROWS = 8
GROUP_HEADS = 4
GROUP = GROUP_HEADS * HEAD_DIM
PAIR = 2 * HEAD_DIM
VMEM_BYTES = 56 * 1024 * 1024
QUICK = pl.CostEstimate(flops=1000000, bytes_accessed=1000000, transcendentals=0)

epsilon = 1e-06
masked_score = -1000000000.0
highest = lax.Precision.HIGHEST
f32 = jnp.float32
bf16 = jnp.bfloat16

NT = (((1,), (1,)), ((), ()))
TN = (((0,), (0,)), ((), ()))


def bucket_limits():
    half_count = BUCKETS // 2
    exact_count = half_count // 2
    lengths = np.arange(exact_count, 4 * MAX_DIST + 2 * LEN + 2)
    levels = (
        np.log(lengths / exact_count) / np.log(MAX_DIST / exact_count) * (half_count - exact_count)
    ).astype(np.int64)
    levels = np.minimum(levels, half_count - exact_count - 1)
    limits = []
    for target in range(1, half_count - exact_count):
        limits.append(int(lengths[np.argmax(levels >= target)]))
    return limits


def bucket_of(distance):
    half_count = BUCKETS // 2
    exact_count = half_count // 2
    magnitude = np.abs(distance)
    counted = np.full(distance.shape, exact_count, np.int32)
    for limit_value in bucket_limits():
        counted = counted + (magnitude >= limit_value).astype(np.int32)
    return np.where(distance > 0, half_count, 0) + np.where(
        magnitude < exact_count, magnitude, counted
    )


def window_buckets():
    place = np.arange(SPAN)
    shift = np.where(place < SIDE, -place, SPAN - place)
    rows = [bucket_of(offset * SIDE + shift) for offset in (-1, 0, 1)]
    for row in rows:
        row[SIDE] = -1
    far = bucket_of(np.array([-2 * SIDE + SIDE - 1, 2 * SIDE - SIDE + 1]))
    rows += [np.full(SPAN, far[0]), np.full(SPAN, far[1])]
    rows += [np.full(SPAN, -1)] * (WINDOW_ROWS - len(rows))
    return np.stack(rows).astype(np.int32)


def window_onehot():
    return (
        jnp.asarray(window_buckets().reshape(-1))[:, None]
        == jnp.arange(BUCKETS, dtype=jnp.int32)[None, :]
    ).astype(f32)


def params(**extra):
    return pltpu.CompilerParams(vmem_limit_bytes=VMEM_BYTES, **extra)


def dot(a, b, dims=None, precision=None):
    if dims is None:
        return jnp.dot(a, b, preferred_element_type=f32, precision=precision)
    return lax.dot_general(a, b, dims, preferred_element_type=f32, precision=precision)


def rms_factor(values):
    return lax.rsqrt(jnp.mean(values * values, axis=-1, keepdims=True) + epsilon)


def half_mask(half):
    lane = lax.broadcasted_iota(jnp.int32, (1, PAIR), 1)
    inside = (lane >= half * HEAD_DIM) & (lane < (half + 1) * HEAD_DIM)
    return inside.astype(f32)


def bias_blocks(windows):
    blocks = {}
    for row, offset in enumerate((-1, 0, 1)):
        spread = jnp.broadcast_to(windows[row : row + 1, :], (SIDE, SPAN))
        blocks[offset] = pltpu.roll(spread, 0, 1, stride=1, stride_axis=0)[:, :SIDE]
    blocks[-2] = jnp.broadcast_to(windows[3:4, :SIDE], (SIDE, SIDE))
    blocks[2] = jnp.broadcast_to(windows[4:5, :SIDE], (SIDE, SIDE))
    return blocks


def offset_of(key_block, query_block):
    return max(-2, min(2, key_block - query_block))


def bias_part(blocks, first_query, width):
    columns = []
    for query_block in range(first_query // SIDE, (first_query + width) // SIDE):
        columns.append(
            jnp.concatenate(
                [blocks[offset_of(key_block, query_block)] for key_block in range(LEN // SIDE)],
                axis=0,
            )
        )
    return jnp.concatenate(columns, axis=1)


def diagonal_sums(block):
    padded = jnp.concatenate([block, jnp.zeros((SIDE, SPAN - SIDE), f32)], axis=1)
    total = padded[:8]
    for first in range(8, SIDE, 8):
        total = total + pltpu.roll(padded[first : first + 8], SPAN - first, 1)
    row = lax.broadcasted_iota(jnp.int32, (8, SPAN), 0)
    for bit in (1, 2, 4):
        total = jnp.where((row & bit) != 0, pltpu.roll(total, SPAN - bit, 1), total)
    return jnp.sum(total, axis=0, keepdims=True)


def mask_of(seg_col, seg_row):
    return jnp.where(seg_col == seg_row, 0.0, masked_score).astype(f32)


def place_matrix(rowid_row, count):
    rows = lax.broadcasted_iota(jnp.int32, (count, rowid_row.shape[1]), 0)
    return (rows == rowid_row).astype(bf16)


def take_matrix(rowid_col, count):
    lanes = lax.broadcasted_iota(jnp.int32, (rowid_col.shape[0], count), 1)
    return (lanes == rowid_col).astype(bf16)


def route_onehot(route_col, experts):
    lanes = lax.broadcasted_iota(jnp.int32, (route_col.shape[0], experts), 1)
    return (lanes == route_col).astype(f32)


def join(refs):
    return jnp.concatenate([ref[...].astype(f32) for ref in refs], axis=0).astype(bf16)


def cut(values, refs):
    count = values.shape[0] // len(refs)
    for index, ref in enumerate(refs):
        ref[...] = values[index * count : (index + 1) * count].astype(ref.dtype)


QUERY_SPAN = 256
SMALL_ROWS = 128


def attend_kernel(layer, experts, refs):
    refs = list(refs)
    take = lambda count: [refs.pop(0) for _ in range(count)]
    combine = layer > 0
    if combine:
        middle_prev, prob_prev, rowcol_prev, route_prev = take(4)
        back_prev = take(experts)
    else:
        (tokens,) = take(1)
    gain_attn, wq, wk, wv, wout, windows, seg_row, seg_col = take(8)
    gain_ffn, router, rowid_row = take(3)
    if combine:
        (x_out,) = take(1)
    proj, mixed, lse, middle, prob = take(5)
    buffer = take(experts)
    normed_s, x_s, acc_s, mask_s = take(4)
    step = pl.program_id(0)

    @pl.when(step == 0)
    def _():
        if combine:
            chosen = route_onehot(route_prev[0], experts)
            gate = jnp.sum(prob_prev[...] * chosen, axis=-1, keepdims=True)
            rows = join(back_prev)
            returned = dot(take_matrix(rowcol_prev[0], rows.shape[0]), rows)
            x = middle_prev[...] + gate * returned
            x_out[...] = x
        else:
            x = tokens[...].astype(f32)
        x_s[...] = x
        normed_s[...] = (x * rms_factor(x) * gain_attn[layer : layer + 1, :]).astype(bf16)
        acc_s[...] = jnp.zeros_like(acc_s)
        mask_s[...] = mask_of(seg_col[...], seg_row[...])

    normed = normed_s[...]
    q = dot(normed, wq[0]).astype(bf16)
    k = dot(normed, wk[0]).astype(bf16)
    v = dot(normed, wv[0]).astype(bf16)
    proj[0] = q
    proj[1] = k
    proj[2] = v
    for pair in range(GROUP_HEADS // 2):
        lanes = slice(pair * PAIR, (pair + 1) * PAIR)
        q2 = q[:, lanes].astype(f32) * HEAD_DIM ** (-0.5)
        k2 = k[:, lanes]
        v2t = v[:, lanes].T
        outs = []
        for half in range(2):
            head = pair * 2 + half
            qm = (q2 * half_mask(half)).astype(bf16)
            vt = v2t[half * HEAD_DIM : (half + 1) * HEAD_DIM, :]
            blocks = bias_blocks(windows[0, head])
            parts = []
            for first in range(0, LEN, QUERY_SPAN):
                span = slice(first, first + QUERY_SPAN)
                scores = dot(k2, qm[span], NT)
                scores = scores + bias_part(blocks, first, QUERY_SPAN) + mask_s[:, span]
                top = jnp.max(scores, axis=0, keepdims=True)
                powers = jnp.exp(scores - top)
                total = jnp.sum(powers, axis=0, keepdims=True)
                parts.append(dot(vt, powers.astype(bf16)) * (1.0 / total))
                lse[0, head : head + 1, span] = top + jnp.log(total)
            outs.append(jnp.concatenate(parts, axis=1))
        mixed[:, lanes] = jnp.concatenate(outs, axis=0).T.astype(bf16)
    acc_s[...] += dot(mixed[...], wout[0])

    @pl.when(step == pl.num_programs(0) - 1)
    def _():
        mid = x_s[...] + acc_s[...]
        middle[...] = mid
        nf = (mid * rms_factor(mid) * gain_ffn[layer : layer + 1, :]).astype(bf16)
        logits = dot(nf.astype(f32), router[0], precision=highest)
        powers = jnp.exp(logits - jnp.max(logits, axis=-1, keepdims=True))
        prob[...] = powers / jnp.sum(powers, axis=-1, keepdims=True)
        cut(dot(place_matrix(rowid_row[0], experts * buffer[0].shape[0]), nf), buffer)


def whole(array):
    zeros = (0,) * array.ndim
    return pl.BlockSpec(array.shape, lambda g: zeros)


def whole_shape(shape):
    zeros = (0,) * len(shape)
    return pl.BlockSpec(shape, lambda g: zeros)


def of_layer(array, layer):
    place = (layer,) + (0,) * (array.ndim - 1)
    return pl.BlockSpec((1,) + array.shape[1:], lambda g: place)


def qkv_specs(width, layer):
    per = width // GROUP
    return [
        pl.BlockSpec(
            (1, width, GROUP), functools.partial(lambda part, g: (layer, 0, part * per + g), part)
        )
        for part in range(3)
    ]


def group_specs(width, layer):
    return (
        pl.BlockSpec((1, GROUP, width), lambda g: (layer, g, 0)),
        pl.BlockSpec((1, GROUP_HEADS, WINDOW_ROWS, SPAN), lambda g: (layer, g, 0, 0)),
    )


def attend(layer, source, common):
    qkv_w, router = common["qkv_w"], common["router"]
    width = qkv_w.shape[1]
    groups = width // GROUP
    experts = router.shape[2]
    out_spec, window_spec = group_specs(width, layer)
    ins, specs = [], []

    def add(array, spec=None):
        ins.append(array)
        specs.append(whole(array) if spec is None else spec)

    if layer > 0:
        add(source["middle"])
        add(source["prob"])
        for name in ("rowcol", "route"):
            add(common[name], of_layer(common[name], layer - 1))
        for block in source["back"]:
            add(block)
    else:
        add(source)
    add(common["gain_attn"])
    for spec in qkv_specs(width, layer):
        add(qkv_w, spec)
    add(common["out_w"], out_spec)
    add(common["windows"], window_spec)
    add(common["seg_row"])
    add(common["seg_col"])
    add(common["gain_ffn"])
    add(router, of_layer(router, layer))
    add(common["rowrow"], of_layer(common["rowrow"], layer))
    block = (common["capacity"], width)
    shapes = [
        ((3, LEN, width), bf16, pl.BlockSpec((3, LEN, GROUP), lambda g: (0, 0, g))),
        ((LEN, width), bf16, pl.BlockSpec((LEN, GROUP), lambda g: (0, g))),
        ((groups, 8, LEN), f32, pl.BlockSpec((1, 8, LEN), lambda g: (g, 0, 0))),
        ((LEN, width), f32, whole_shape((LEN, width))),
        ((LEN, experts), f32, whole_shape((LEN, experts))),
    ] + [(block, bf16, whole_shape(block))] * experts
    if layer > 0:
        shapes = [((LEN, width), f32, whole_shape((LEN, width)))] + shapes
    return pl.pallas_call(
        lambda *refs: attend_kernel(layer, experts, refs),
        grid=(groups,),
        in_specs=specs,
        out_specs=[s[2] for s in shapes],
        out_shape=[jax.ShapeDtypeStruct(s[0], s[1]) for s in shapes],
        scratch_shapes=[
            pltpu.VMEM((LEN, width), bf16),
            pltpu.VMEM((LEN, width), f32),
            pltpu.VMEM((LEN, width), f32),
            pltpu.VMEM((LEN, LEN), f32),
        ],
        compiler_params=params(),
        cost_estimate=QUICK,
        name="attend",
    )(*ins)


def attend_back_kernel(layer, experts, refs):
    refs = list(refs)
    take = lambda count: [refs.pop(0) for _ in range(count)]
    first_layer = layer == 0
    gradient, rowcol, gate_grad, prob, route_col, middle, gain_ffn, router = take(8)
    gback = take(experts)
    x_ref, gain_attn, wq, wk, wv, wout, proj, mixed, lse, windows, seg_row, seg_col, onehot = take(13)
    if not first_layer:
        rowrow_prev, rowcol_prev, prob_prev, route_prev = take(4)
        back_prev = take(experts)
    grad_in, big = take(2)
    if not first_layer:
        (gate_grad_prev,) = take(1)
        buffer_prev = take(experts)
    normt_s, mg_s, att_s, acc_s, mask_s, small_s, rel_s = take(7)
    step = pl.program_id(0)
    width = att_s.shape[1]
    places = dict(
        q=0, k=width, small=2 * width, v=2 * width + SMALL_ROWS, out=3 * width + SMALL_ROWS
    )
    columns = pl.ds(pl.multiple_of(step * GROUP, GROUP), GROUP)

    @pl.when(step == 0)
    def _():
        g = gradient[...].astype(f32)
        rows = join(gback)
        expert_part = dot(take_matrix(rowcol[0], rows.shape[0]), rows)
        probability = prob[...]
        chosen = route_onehot(route_col[0], experts)
        gate = jnp.sum(probability * chosen, axis=-1, keepdims=True)
        logit_grad = gate_grad[...] * gate * (chosen - probability)
        mid = middle[...]
        r = rms_factor(mid)
        scaled = mid * r
        gain = gain_ffn[layer : layer + 1, :]
        nf = (scaled * gain).astype(bf16).astype(f32)
        small_s[...] = jnp.zeros_like(small_s)
        small_s[:experts] = dot(logit_grad, nf, TN, precision=highest)
        ffn_in = expert_part + dot(logit_grad, router[0], NT, precision=highest)
        u = ffn_in * gain
        mg = g + r * (u - scaled * (r * jnp.mean(u * mid, axis=-1, keepdims=True)))
        small_s[experts + 1 : experts + 2] = jnp.sum(ffn_in * scaled, axis=0, keepdims=True)
        mg_s[...] = mg
        att_s[...] = mg.astype(bf16)
        x = x_ref[...].astype(f32)
        normed = (x * rms_factor(x) * gain_attn[layer : layer + 1, :]).astype(bf16)
        normt_s[...] = normed.T
        acc_s[...] = jnp.zeros_like(acc_s)
        mask_s[...] = mask_of(seg_col[...], seg_row[...])

    att = att_s[...]
    out_rows = pl.ds(pl.multiple_of(places["out"] + step * GROUP, SMALL_ROWS), GROUP)
    big[out_rows, :] = dot(mixed[...], att, TN).astype(big.dtype)
    mixed_grad = dot(att, wout[0], NT).astype(bf16)
    dqs, dks, dvs, rel_rows = [], [], [], []
    for pair in range(GROUP_HEADS // 2):
        lanes = slice(pair * PAIR, (pair + 1) * PAIR)
        q2 = proj[0, :, lanes].astype(f32) * HEAD_DIM ** (-0.5)
        k2 = proj[1, :, lanes]
        v2 = proj[2, :, lanes]
        k2t = k2.T
        o2 = mixed_grad[:, lanes].astype(f32)
        dk = jnp.zeros((LEN, PAIR), f32)
        dv = jnp.zeros((LEN, PAIR), f32)
        dqts = []
        for half in range(2):
            head = pair * 2 + half
            qm = (q2 * half_mask(half)).astype(bf16)
            om = (o2 * half_mask(half)).astype(bf16)
            kt = k2t[half * HEAD_DIM : (half + 1) * HEAD_DIM, :]
            blocks = bias_blocks(windows[0, head])
            sums = {}
            parts = []
            for first in range(0, LEN, QUERY_SPAN):
                span = slice(first, first + QUERY_SPAN)
                scores = dot(k2, qm[span], NT)
                scores = scores + bias_part(blocks, first, QUERY_SPAN) + mask_s[:, span]
                powers = jnp.exp(scores - lse[0, head : head + 1, span])
                prob_grad = dot(v2, om[span], NT)
                weighted = powers * prob_grad
                delta = jnp.sum(weighted, axis=0, keepdims=True)
                score_grad = weighted - powers * delta
                for kb in range(LEN // SIDE):
                    for qb in range(QUERY_SPAN // SIDE):
                        piece = score_grad[kb * SIDE : (kb + 1) * SIDE, qb * SIDE : (qb + 1) * SIDE]
                        offset = offset_of(kb, qb + first // SIDE)
                        sums[offset] = sums[offset] + piece if offset in sums else piece
                sg = score_grad.astype(bf16)
                dv = dv + dot(powers.astype(bf16), om[span])
                dk = dk + dot(sg, qm[span])
                parts.append(dot(kt, sg))
            dqts.append(jnp.concatenate(parts, axis=1))
            rel_rows.append(
                [diagonal_sums(sums[offset]) for offset in (-1, 0, 1)]
                + [
                    jnp.concatenate(
                        [jnp.sum(sums[offset], axis=0, keepdims=True)] + [jnp.zeros((1, SPAN - SIDE), f32)],
                        axis=1,
                    )
                    for offset in (-2, 2)
                ]
            )
        dqs.append((jnp.concatenate(dqts, axis=0) * HEAD_DIM ** (-0.5)).T)
        dks.append(dk)
        dvs.append(dv)
    total = acc_s[...]
    for name, weight, pieces in (("q", wq, dqs), ("k", wk, dks), ("v", wv, dvs)):
        part = jnp.concatenate(pieces, axis=1).astype(bf16)
        first = places[name]
        big[first : first + width, columns] = dot(normt_s[...], part).astype(big.dtype)
        total = total + dot(part, weight[0], NT)
    acc_s[...] = total
    for group in range(width // GROUP):

        @pl.when(step == group)
        def _(group=group):
            for index, rows in enumerate(rel_rows):
                at = group * GROUP_HEADS + index
                for kind, row in enumerate(rows):
                    rel_s[kind, at : at + 1, :] = row

    @pl.when(step == pl.num_programs(0) - 1)
    def _():
        x = x_ref[...].astype(f32)
        r = rms_factor(x)
        scaled = x * r
        attn_in = acc_s[...]
        u = attn_in * gain_attn[layer : layer + 1, :]
        g = mg_s[...] + r * (u - scaled * (r * jnp.mean(u * x, axis=-1, keepdims=True)))
        small_s[experts : experts + 1] = jnp.sum(attn_in * scaled, axis=0, keepdims=True)
        heads = width // HEAD_DIM
        bucket_sums = jnp.zeros((heads, BUCKETS), f32)
        for kind in range(5):
            bucket_sums = bucket_sums + dot(
                rel_s[kind], onehot[kind * SPAN : (kind + 1) * SPAN], precision=highest
            )
        small_s[experts + 2 : experts + 2 + heads, :BUCKETS] = bucket_sums
        big[places["small"] : places["small"] + SMALL_ROWS, :] = small_s[...].astype(big.dtype)
        big[places["out"] + width :, :] = jnp.zeros((SMALL_ROWS, width), big.dtype)
        grad_in[...] = g
        if not first_layer:
            send_back(
                g, back_prev, rowrow_prev, rowcol_prev, prob_prev, route_prev, buffer_prev, gate_grad_prev
            )


def send_back(g, back, rowrow, rowcol, prob, route_col, buffer, gate_grad):
    rows = join(back)
    returned = dot(take_matrix(rowcol[0], rows.shape[0]), rows)
    chosen = route_onehot(route_col[0], prob.shape[1])
    gate = jnp.sum(prob[...] * chosen, axis=-1, keepdims=True)
    gate_grad[...] = jnp.sum(g * returned, axis=-1, keepdims=True)
    expert_grad = (gate * g).astype(bf16)
    cut(dot(place_matrix(rowrow[0], rows.shape[0]), expert_grad), buffer)
    return gate * returned


def attend_back(layer, states, gradient, gback, gate_grad, common):
    state = states[layer]
    qkv_w, router = common["qkv_w"], common["router"]
    width = qkv_w.shape[1]
    groups = width // GROUP
    experts = router.shape[2]
    out_spec, window_spec = group_specs(width, layer)
    ins, specs = [], []

    def add(array, spec=None):
        ins.append(array)
        specs.append(whole(array) if spec is None else spec)

    add(gradient)
    add(common["rowcol"], of_layer(common["rowcol"], layer))
    add(gate_grad)
    add(state["prob"])
    add(common["route"], of_layer(common["route"], layer))
    add(state["middle"])
    add(common["gain_ffn"])
    add(router, of_layer(router, layer))
    for block in gback:
        add(block)
    add(state["x"])
    add(common["gain_attn"])
    for spec in qkv_specs(width, layer):
        add(qkv_w, spec)
    add(common["out_w"], out_spec)
    add(state["proj"], pl.BlockSpec((3, LEN, GROUP), lambda g: (0, 0, g)))
    add(state["mixed"], pl.BlockSpec((LEN, GROUP), lambda g: (0, g)))
    add(state["lse"], pl.BlockSpec((1, 8, LEN), lambda g: (g, 0, 0)))
    add(common["windows"], window_spec)
    add(common["seg_row"])
    add(common["seg_col"])
    add(common["onehot"])
    payload = (4 * width + 2 * SMALL_ROWS, width)
    shapes = [((LEN, width), f32), (payload, bf16)]
    if layer > 0:
        for name in ("rowrow", "rowcol"):
            add(common[name], of_layer(common[name], layer - 1))
        add(states[layer - 1]["prob"])
        add(common["route"], of_layer(common["route"], layer - 1))
        for block in states[layer - 1]["back"]:
            add(block)
        shapes += [((LEN, 1), f32)] + [((common["capacity"], width), bf16)] * experts
    return pl.pallas_call(
        lambda *refs: attend_back_kernel(layer, experts, refs),
        grid=(groups,),
        in_specs=specs,
        out_specs=[whole_shape(s[0]) for s in shapes],
        out_shape=[jax.ShapeDtypeStruct(s[0], s[1]) for s in shapes],
        scratch_shapes=[
            pltpu.VMEM((width, LEN), bf16),
            pltpu.VMEM((LEN, width), f32),
            pltpu.VMEM((LEN, width), bf16),
            pltpu.VMEM((LEN, width), f32),
            pltpu.VMEM((LEN, LEN), f32),
            pltpu.VMEM((SMALL_ROWS, width), f32),
            pltpu.VMEM((5, width // HEAD_DIM, SPAN), f32),
        ],
        compiler_params=params(),
        cost_estimate=QUICK,
        name="attend_back",
    )(*ins)


def turn_kernel(experts, refs):
    middle, cotangent, rowrow, rowcol, prob, route_col = refs[:6]
    back = refs[6 : 6 + experts]
    output, gate_grad = refs[6 + experts : 8 + experts]
    buffer = refs[8 + experts :]
    g = cotangent[...].astype(f32)
    added = send_back(g, back, rowrow, rowcol, prob, route_col, buffer, gate_grad)
    output[...] = middle[...] + added


def turn(layer, state, cotangent, common):
    width = cotangent.shape[1]
    experts = len(state["back"])
    ins = [state["middle"], cotangent, common["rowrow"], common["rowcol"], state["prob"]]
    ins += [common["route"]] + list(state["back"])
    specs = [whole(array) for array in ins]
    for index in (2, 3, 5):
        specs[index] = of_layer(ins[index], layer)
    shapes = [((LEN, width), f32), ((LEN, 1), f32)]
    shapes += [((common["capacity"], width), bf16)] * experts
    return pl.pallas_call(
        lambda *refs: turn_kernel(experts, refs),
        grid=(1,),
        in_specs=specs,
        out_specs=[whole_shape(s[0]) for s in shapes],
        out_shape=[jax.ShapeDtypeStruct(s[0], s[1]) for s in shapes],
        compiler_params=params(),
        cost_estimate=QUICK,
        name="turn",
    )(*ins)


GELU_A = float(np.sqrt(2.0 / np.pi))
GELU_B = 0.044715


def gelu_tanh(hidden):
    return jnp.tanh(GELU_A * (hidden + GELU_B * (hidden * hidden * hidden)))


def gelu_of(hidden, curve):
    return 0.5 * hidden * (1.0 + curve)


def gelu_slope(hidden, curve):
    inner = GELU_A * (1.0 + (3.0 * GELU_B) * (hidden * hidden))
    return 0.5 * (1.0 + curve) + 0.5 * hidden * (1.0 - curve * curve) * inner


def expert_kernel(experts, refs):
    blocks = refs[:experts]
    w_in, w_out, rows = refs[experts : experts + 3]
    outs = refs[experts + 3 : -1]
    acc = refs[-1]
    step = pl.program_id(0)

    @pl.when(step == 0)
    def _():
        rows[...] = join(blocks)
        acc[...] = jnp.zeros_like(acc)

    hidden = dot(rows[...], w_in[...])
    active = gelu_of(hidden, gelu_tanh(hidden)).astype(bf16)
    acc[...] += dot(active, w_out[...])

    @pl.when(step == pl.num_programs(0) - 1)
    def _():
        cut(acc[...], outs)


def weight_specs(weights):
    if len(weights) == 1:
        width = weights[0].shape[1]
        return [
            pl.BlockSpec((width, width), lambda b: (2 * b, 0)),
            pl.BlockSpec((width, width), lambda b: (2 * b + 1, 0)),
        ]
    parts = weights[0].shape[0] // weights[1].shape[1]
    return [
        pl.BlockSpec((array.shape[0] // parts, array.shape[1]), lambda b: (b, 0))
        for array in weights
    ]


def expert(blocks, weights, parts):
    experts = len(blocks)
    capacity, width = blocks[0].shape
    count = experts * capacity
    rows_shape = jax.ShapeDtypeStruct((count, width), bf16)
    specs = [whole(block) for block in blocks]
    hidden = weights[-1].shape[0] // (2 if len(weights) == 1 else 1)
    results = pl.pallas_call(
        lambda *refs: expert_kernel(experts, refs),
        grid=(parts,),
        in_specs=specs + weight_specs(weights),
        out_specs=[whole_shape((count, width))] + specs,
        out_shape=[rows_shape] + [jax.ShapeDtypeStruct(b.shape, bf16) for b in blocks],
        scratch_shapes=[pltpu.VMEM((count, width), f32)],
        compiler_params=params(),
        cost_estimate=QUICK,
        name="expert",
    )(*blocks, *(weights * 2)[:2])
    return results[0], results[1:]


def expert_back_kernel(experts, refs):
    rows = refs[0]
    blocks = refs[1 : 1 + experts]
    w_in, w_out, grads = refs[1 + experts : 4 + experts]
    outs = refs[4 + experts : -1]
    acc = refs[-1]
    step = pl.program_id(0)

    @pl.when(step == 0)
    def _():
        grads[...] = join(blocks)
        acc[...] = jnp.zeros_like(acc)

    hidden = dot(rows[...], w_in[...])
    act_grad = dot(grads[...], w_out[...], NT)
    pre_grad = (act_grad * gelu_slope(hidden, gelu_tanh(hidden))).astype(bf16)
    acc[...] += dot(pre_grad, w_in[...], NT)

    @pl.when(step == pl.num_programs(0) - 1)
    def _():
        cut(acc[...], outs)


def expert_back(rows, blocks, weights, parts):
    experts = len(blocks)
    count, width = rows.shape
    specs = [whole(block) for block in blocks]
    hidden = weights[-1].shape[0] // (2 if len(weights) == 1 else 1)
    results = pl.pallas_call(
        lambda *refs: expert_back_kernel(experts, refs),
        grid=(parts,),
        in_specs=[whole(rows)] + specs + weight_specs(weights),
        out_specs=[whole(rows)] + specs,
        out_shape=[jax.ShapeDtypeStruct(a.shape, bf16) for a in [rows] + list(blocks)],
        scratch_shapes=[pltpu.VMEM((count, width), f32)],
        compiler_params=params(),
        cost_estimate=QUICK,
        name="expert_back",
    )(rows, *blocks, *(weights * 2)[:2])
    return results[0], results[1:]


def weight_grad_kernel(order, rows, grads, w_in, w_out, *refs):
    g_in, g_out = refs[-2:]
    step = pl.program_id(0)

    @pl.when(step == 0)
    def _():
        g_in[...] = jnp.zeros_like(g_in)
        g_out[...] = jnp.zeros_like(g_out)

    hidden = dot(rows[...], w_in[0, 0])
    curve = gelu_tanh(hidden)
    active = gelu_of(hidden, curve).astype(bf16)
    act_grad = dot(grads[...], w_out[0, 0], NT)
    pre_grad = (act_grad * gelu_slope(hidden, curve)).astype(bf16)
    g_out[0, 0] += dot(active, grads[...], TN)
    g_in[0, 0] += dot(rows[...], pre_grad, TN)


def weight_grad(layer, order, rows_all, grads_all, w_in, w_out, into):
    width = w_in.shape[2]
    parts = order.shape[0]
    count = rows_all.shape[0] // parts

    def part_of(array):
        return pl.BlockSpec((1, 1) + array.shape[2:], lambda b, order: (layer, 0, 0, 0))

    specs = [part_of(w_in), part_of(w_out)]
    grid_spec = pltpu.PrefetchScalarGridSpec(
        num_scalar_prefetch=1,
        grid=(parts,),
        in_specs=[
            pl.BlockSpec((count, width), lambda b, order: (order[b], 0)),
            pl.BlockSpec((count, width), lambda b, order: (b, 0)),
        ]
        + specs
        + [pl.BlockSpec(memory_space=pl.ANY)] * len(into),
        out_specs=specs,
    )
    return pl.pallas_call(
        weight_grad_kernel,
        grid_spec=grid_spec,
        out_shape=[
            jax.ShapeDtypeStruct(w_in.shape, f32),
            jax.ShapeDtypeStruct(w_out.shape, f32),
        ],
        input_output_aliases={5 + index: index for index in range(len(into))},
        compiler_params=params(),
        cost_estimate=QUICK,
        name="weight_grad",
    )(order, rows_all, grads_all, w_in, w_out, *into)


def finish_kernel(side, first, second, qkv, out):
    kind = pl.program_id(0) % 4
    upper = (side[0] + jnp.where(kind >= 2, 1, 0)) % 2
    values = jnp.where(upper == 0, first[...].astype(f32), second[...].astype(f32))

    @pl.when(kind < 3)
    def _():
        qkv[0] = values

    @pl.when(kind == 3)
    def _():
        out[0] = values


def finish(side, first, second):
    width = first.shape[1] // LAYERS

    def rows_of(turned):
        def place(step, side):
            kind = step % 4
            lower, higher = jnp.minimum(kind, 1), jnp.maximum(kind, 2) - 2
            return jnp.where(side[0] == turned, lower, higher), step // 4

        return pl.BlockSpec((width, width), place)

    grid_spec = pltpu.PrefetchScalarGridSpec(
        num_scalar_prefetch=1,
        grid=(4 * LAYERS,),
        in_specs=[rows_of(0), rows_of(1)],
        out_specs=[
            pl.BlockSpec(
                (1, width, width), lambda step, side: (step // 4, 0, jnp.minimum(step % 4, 2))
            ),
            pl.BlockSpec((1, width, width), lambda step, side: (step // 4, 0, 0)),
        ],
    )
    return pl.pallas_call(
        finish_kernel,
        grid_spec=grid_spec,
        out_shape=[
            jax.ShapeDtypeStruct((LAYERS, width, 3 * width), f32),
            jax.ShapeDtypeStruct((LAYERS, width, width), f32),
        ],
        compiler_params=params(),
        cost_estimate=QUICK,
        name="finish",
    )(side.reshape(1), first, second)


def partner(array, axis, bit):
    pairs = [(index, index ^ bit) for index in range(lax.axis_size(axis))]
    return lax.ppermute(array, axis, pairs)


def swap(blocks):
    return [blocks[0]] + [partner(block, "dp", k) for k, block in enumerate(blocks) if k > 0]


def gather_rows(rows):
    return lax.all_gather(rows, "mp", axis=0, tiled=True)


def gather_weights(w_in, w_out, layer):
    first, second = w_in[layer, 0], w_out[layer, 0]
    if first.shape == second.shape:
        joined = jnp.concatenate([first, second], axis=0)
        return (lax.all_gather(joined, "mp", axis=0, tiled=True),)
    return tuple(lax.all_gather(part, "mp", axis=0, tiled=True) for part in (first, second))


def bit_of(step):
    axis, bit = step
    return (lax.axis_index(axis) // bit) % 2


def add_rounded(kept, received):
    return (kept.astype(f32) + received.astype(f32)).astype(kept.dtype)


def halve(array, step):
    half = array.shape[0] // 2
    mine = bit_of(step)
    kept = lax.dynamic_slice_in_dim(array, mine * half, half, 0)
    sent = lax.dynamic_slice_in_dim(array, (1 - mine) * half, half, 0)
    return kept, sent


def bits_of(axis):
    size = lax.axis_size(axis)
    return [(axis, 1 << place) for place in range(size.bit_length() - 1)]


def sum_of_cores(payload):
    core = bits_of("dp")[0]
    kept, sent = halve(payload, core)
    return add_rounded(kept, partner(sent, *core))


def sum_everywhere(total, beside):
    along_dp, along_mp = bits_of("dp"), bits_of("mp")
    core, along_z = along_dp[0], along_dp[1:]
    half_mp = len(along_mp) // 2
    inner, outer = along_mp[:half_mp], along_mp[half_mp:]
    near, far = along_z[:1], along_z[1:]
    orders = [inner + outer + near + far, outer + near + inner + far, near + inner + outer + far]
    unit = 1 << len(orders[0])
    units = total.shape[0] // unit
    sizes = [(units + 2 - index) // 3 * unit for index in range(3)]
    starts = [0, sizes[0], sizes[0] + sizes[1]]
    parts = [total[start : start + size] for start, size in zip(starts, sizes)]
    for level in range(len(orders[0])):
        steps = [order[level] for order in orders]
        halves = [halve(part, step) for part, step in zip(parts, steps)]
        received = [partner(half[1], *step) for half, step in zip(halves, steps)]
        received = lax.optimization_barrier(received)
        if level == 0:
            received, beside = lax.optimization_barrier((received, beside))
        parts = [add_rounded(half[0], other) for half, other in zip(halves, received)]
        parts = lax.optimization_barrier(parts)
    for level in reversed(range(len(orders[0]))):
        steps = [order[level] for order in orders]
        received = [partner(part, *step) for part, step in zip(parts, steps)]
        received = lax.optimization_barrier(received)
        parts = [
            jnp.where(
                bit_of(step) == 0,
                jnp.concatenate([part, other], axis=0),
                jnp.concatenate([other, part], axis=0),
            )
            for part, other, step in zip(parts, received, steps)
        ]
    mine = jnp.concatenate(parts, axis=0)
    return mine, partner(mine, *core), beside


def body(
    tokens,
    segments,
    routes,
    gain_attn,
    qkv_weight,
    out_weight,
    rel_bias,
    gain_ffn,
    router_weight,
    w_in,
    w_out,
    cotangent,
):
    tok_count, width = tokens.shape
    experts = w_in.shape[1] * lax.axis_size("dp")
    parts = lax.axis_size("mp")
    capacity = (tok_count * 9 + 8 * experts - 1) // (8 * experts)
    heads = width // HEAD_DIM

    weights = [gather_weights(w_in, w_out, layer) for layer in range(LAYERS)]
    onehot = window_onehot()
    windows = jnp.einsum("pb,lbh->lhp", onehot, rel_bias, precision=highest)
    chosen = routes[:, :, 0]
    chosen_onehot = (
        chosen[:, :, None] == jnp.arange(experts, dtype=jnp.int32)[None, None, :]
    ).astype(jnp.int32)
    slots = jnp.sum(jnp.cumsum(chosen_onehot, axis=1) * chosen_onehot, axis=-1) - 1
    rowid = (chosen ^ lax.axis_index("dp")) * capacity + slots
    common = dict(
        gain_attn=gain_attn,
        gain_ffn=gain_ffn,
        qkv_w=qkv_weight,
        out_w=out_weight,
        router=router_weight,
        windows=windows.reshape(LAYERS, heads, WINDOW_ROWS, SPAN),
        onehot=onehot,
        seg_row=segments.reshape(1, LEN),
        seg_col=segments.reshape(LEN, 1),
        rowrow=rowid[:, None, :],
        rowcol=rowid[:, :, None],
        route=routes,
        capacity=capacity,
    )

    states = []
    source = tokens
    for layer in range(LAYERS):
        results = list(attend(layer, source, common))
        state = dict(x=results.pop(0) if layer > 0 else tokens)
        for name in ("proj", "mixed", "lse", "middle", "prob"):
            state[name] = results.pop(0)
        state["rows"], outs = expert(swap(results), weights[layer], parts)
        state["back"] = swap(outs)
        states.append(state)
        source = state

    rows_all = [gather_rows(state["rows"]) for state in states]
    output, gate_grad, *blocks = turn(LAYERS - 1, states[-1], cotangent, common)
    gradient = cotangent
    totals = [None] * LAYERS
    order = jnp.arange(parts, dtype=jnp.int32)
    weight_grads = ()
    for layer in reversed(range(LAYERS)):
        last = layer == 0
        arrived = swap(blocks)
        if layer == LAYERS - 1:
            arrived, rows_all[0] = lax.optimization_barrier((arrived, rows_all[0]))
        else:
            arrived, weight_grads = lax.optimization_barrier((arrived, weight_grads))
        grads, sent = expert_back(states[layer]["rows"], arrived, weights[layer], parts)
        gback = swap(sent)
        if layer > 0:
            gback, rows_all[layer] = lax.optimization_barrier((gback, rows_all[layer]))
        grads_all = gather_rows(grads)
        results = attend_back(layer, states, gradient, gback, gate_grad, common)
        gradient, payload = results[:2]
        if layer > 0:
            gate_grad, *blocks = results[2:]
            totals[layer] = sum_of_cores(payload)
        else:
            payload, grads_all = lax.optimization_barrier((payload, grads_all))
            totals[layer] = sum_of_cores(payload)
            totals[layer], grads_all = lax.optimization_barrier((totals[layer], grads_all))
        weight_grads = weight_grad(
            layer, order, rows_all[layer], grads_all, w_in, w_out, tuple(weight_grads)
        )
    total = jnp.concatenate(totals, axis=1)
    mine, other, (grad_w_in, grad_w_out) = sum_everywhere(total, weight_grads)
    side = lax.axis_index("dp").astype(jnp.int32) % 2
    grad_qkv, grad_out = finish(side, mine, other)
    rows = jnp.where(side == 0, mine[2 * width :], other[2 * width :]).astype(f32)
    small = [rows[:, layer * width : (layer + 1) * width] for layer in range(LAYERS)]
    grad_gain_attn = jnp.stack([rows[experts] for rows in small])
    grad_gain_ffn = jnp.stack([rows[experts + 1] for rows in small])
    grad_router = jnp.stack([rows[:experts].T for rows in small])
    grad_rel = jnp.stack([rows[experts + 2 : experts + 2 + heads, :BUCKETS].T for rows in small])
    return (
        output,
        gradient,
        grad_gain_attn,
        grad_qkv,
        grad_out,
        grad_rel,
        grad_gain_ffn,
        grad_router,
        grad_w_in,
        grad_w_out,
    )


def solution(mesh):
    return jax.shard_map(
        body,
        mesh=mesh,
        in_specs=(
            P(("dp", "mp"), None),
            P(("dp", "mp"), None),
            P(None, ("dp", "mp"), None),
            P(),
            P(),
            P(),
            P(),
            P(),
            P(),
            P(None, "dp", None, "mp"),
            P(None, "dp", "mp", None),
            P(("dp", "mp"), None),
        ),
        out_specs=(
            P(("dp", "mp"), None),
            P(("dp", "mp"), None),
            P(),
            P(),
            P(),
            P(),
            P(),
            P(),
            P(None, "dp", None, "mp"),
            P(None, "dp", "mp", None),
        ),
        check_vma=False,
    )
```

```python
import functools

import jax
import jax.numpy as jnp
import numpy as np
from jax import lax
from jax.experimental import pallas as pl
from jax.experimental.pallas import tpu as pltpu
from jax.sharding import PartitionSpec as P

HEAD_DIM = 64
BUCKETS = 32
MAX_DIST = 128
LAYERS = 2
LEN = 512

SIDE = 128
SPAN = 256
WINDOW_ROWS = 8
GROUP_HEADS = 4
GROUP = GROUP_HEADS * HEAD_DIM
PAIR = 2 * HEAD_DIM
VMEM_BYTES = 56 * 1024 * 1024
QUICK = pl.CostEstimate(flops=1000000, bytes_accessed=1000000, transcendentals=0)

epsilon = 1e-06
masked_score = -1000000000.0
highest = lax.Precision.HIGHEST
f32 = jnp.float32
bf16 = jnp.bfloat16

NT = (((1,), (1,)), ((), ()))
TN = (((0,), (0,)), ((), ()))


def bucket_limits():
    half_count = BUCKETS // 2
    exact_count = half_count // 2
    lengths = np.arange(exact_count, 4 * MAX_DIST + 2 * LEN + 2)
    levels = (
        np.log(lengths / exact_count) / np.log(MAX_DIST / exact_count) * (half_count - exact_count)
    ).astype(np.int64)
    levels = np.minimum(levels, half_count - exact_count - 1)
    limits = []
    for target in range(1, half_count - exact_count):
        limits.append(int(lengths[np.argmax(levels >= target)]))
    return limits


def bucket_of(distance):
    half_count = BUCKETS // 2
    exact_count = half_count // 2
    magnitude = np.abs(distance)
    counted = np.full(distance.shape, exact_count, np.int32)
    for limit_value in bucket_limits():
        counted = counted + (magnitude >= limit_value).astype(np.int32)
    return np.where(distance > 0, half_count, 0) + np.where(
        magnitude < exact_count, magnitude, counted
    )


def window_buckets():
    place = np.arange(SPAN)
    shift = np.where(place < SIDE, -place, SPAN - place)
    rows = [bucket_of(offset * SIDE + shift) for offset in (-1, 0, 1)]
    for row in rows:
        row[SIDE] = -1
    far = bucket_of(np.array([-2 * SIDE + SIDE - 1, 2 * SIDE - SIDE + 1]))
    rows += [np.full(SPAN, far[0]), np.full(SPAN, far[1])]
    rows += [np.full(SPAN, -1)] * (WINDOW_ROWS - len(rows))
    return np.stack(rows).astype(np.int32)


def window_onehot():
    return (
        jnp.asarray(window_buckets().reshape(-1))[:, None]
        == jnp.arange(BUCKETS, dtype=jnp.int32)[None, :]
    ).astype(f32)


def params(**extra):
    return pltpu.CompilerParams(vmem_limit_bytes=VMEM_BYTES, **extra)


def dot(a, b, dims=None, precision=None):
    if dims is None:
        return jnp.dot(a, b, preferred_element_type=f32, precision=precision)
    return lax.dot_general(a, b, dims, preferred_element_type=f32, precision=precision)


def pieces_of(values):
    first = values.astype(bf16)
    rest = values - first.astype(f32)
    second = rest.astype(bf16)
    return first, second, (rest - second.astype(f32)).astype(bf16)


def rms_factor(values):
    return lax.rsqrt(jnp.mean(values * values, axis=-1, keepdims=True) + epsilon)


def half_mask(half):
    lane = lax.broadcasted_iota(jnp.int32, (1, PAIR), 1)
    inside = (lane >= half * HEAD_DIM) & (lane < (half + 1) * HEAD_DIM)
    return inside.astype(f32)


def bias_blocks(windows):
    blocks = {}
    for row, offset in enumerate((-1, 0, 1)):
        spread = jnp.broadcast_to(windows[row : row + 1, :], (SIDE, SPAN))
        blocks[offset] = pltpu.roll(spread, 0, 1, stride=1, stride_axis=0)[:, :SIDE]
    blocks[-2] = jnp.broadcast_to(windows[3:4, :SIDE], (SIDE, SIDE))
    blocks[2] = jnp.broadcast_to(windows[4:5, :SIDE], (SIDE, SIDE))
    return blocks


def offset_of(key_block, query_block):
    return max(-2, min(2, key_block - query_block))


def bias_part(blocks, first_query, width):
    columns = []
    for query_block in range(first_query // SIDE, (first_query + width) // SIDE):
        columns.append(
            jnp.concatenate(
                [blocks[offset_of(key_block, query_block)] for key_block in range(LEN // SIDE)],
                axis=0,
            )
        )
    return jnp.concatenate(columns, axis=1)


def diagonal_sums(block):
    padded = jnp.concatenate([block, jnp.zeros((SIDE, SPAN - SIDE), f32)], axis=1)
    total = padded[:8]
    for first in range(8, SIDE, 8):
        total = total + pltpu.roll(padded[first : first + 8], SPAN - first, 1)
    row = lax.broadcasted_iota(jnp.int32, (8, SPAN), 0)
    for bit in (1, 2, 4):
        total = jnp.where((row & bit) != 0, pltpu.roll(total, SPAN - bit, 1), total)
    return jnp.sum(total, axis=0, keepdims=True)


def mask_of(seg_col, seg_row):
    return jnp.where(seg_col == seg_row, 0.0, masked_score).astype(f32)


def place_matrix(rowid_row, count):
    rows = lax.broadcasted_iota(jnp.int32, (count, rowid_row.shape[1]), 0)
    return (rows == rowid_row).astype(bf16)


def take_matrix(rowid_col, count):
    lanes = lax.broadcasted_iota(jnp.int32, (rowid_col.shape[0], count), 1)
    return (lanes == rowid_col).astype(bf16)


def route_onehot(route_col, experts):
    lanes = lax.broadcasted_iota(jnp.int32, (route_col.shape[0], experts), 1)
    return (lanes == route_col).astype(f32)


def join(refs):
    return jnp.concatenate([ref[...].astype(f32) for ref in refs], axis=0).astype(bf16)


def cut(values, refs):
    count = values.shape[0] // len(refs)
    for index, ref in enumerate(refs):
        ref[...] = values[index * count : (index + 1) * count].astype(ref.dtype)


QUERY_SPAN = 512
SMALL_ROWS = 128


def attend_kernel(layer, experts, refs):
    refs = list(refs)
    take = lambda count: [refs.pop(0) for _ in range(count)]
    combine = layer > 0
    if combine:
        middle_prev, prob_prev, rowcol_prev, route_prev = take(4)
        back_prev = take(experts)
    else:
        (tokens,) = take(1)
    gain_attn, wq, wk, wv, wout, windows, seg_row, seg_col = take(8)
    gain_ffn, router, rowid_row = take(3)
    if combine:
        (x_out,) = take(1)
    proj, mixed, lse, middle, prob = take(5)
    buffer = take(experts)
    normed_s, x_s, acc_s, mask_s = take(4)
    step = pl.program_id(0)

    @pl.when(step == 0)
    def _():
        if combine:
            chosen = route_onehot(route_prev[0], experts)
            gate = jnp.sum(prob_prev[...] * chosen, axis=-1, keepdims=True)
            rows = join(back_prev)
            returned = dot(take_matrix(rowcol_prev[0], rows.shape[0]), rows)
            x = middle_prev[...] + gate * returned
            x_out[...] = x
        else:
            x = tokens[...].astype(f32)
        x_s[...] = x
        normed_s[...] = (x * rms_factor(x) * gain_attn[layer : layer + 1, :]).astype(bf16)
        acc_s[...] = jnp.zeros_like(acc_s)
        mask_s[...] = mask_of(seg_col[...], seg_row[...])

    normed = normed_s[...]
    q = dot(normed, wq[0]).astype(bf16)
    k = dot(normed, wk[0]).astype(bf16)
    v = dot(normed, wv[0]).astype(bf16)
    proj[0] = q
    proj[1] = k
    proj[2] = v
    for pair in range(GROUP_HEADS // 2):
        lanes = slice(pair * PAIR, (pair + 1) * PAIR)
        q2 = q[:, lanes].astype(f32) * HEAD_DIM ** (-0.5)
        k2 = k[:, lanes]
        v2t = v[:, lanes].T
        outs = []
        for half in range(2):
            head = pair * 2 + half
            qm = (q2 * half_mask(half)).astype(bf16)
            vt = v2t[half * HEAD_DIM : (half + 1) * HEAD_DIM, :]
            blocks = bias_blocks(windows[0, head])
            parts = []
            for first in range(0, LEN, QUERY_SPAN):
                span = slice(first, first + QUERY_SPAN)
                scores = dot(k2, qm[span], NT)
                scores = scores + bias_part(blocks, first, QUERY_SPAN) + mask_s[:, span]
                top = jnp.max(scores, axis=0, keepdims=True)
                powers = jnp.exp(scores - top)
                total = jnp.sum(powers, axis=0, keepdims=True)
                parts.append(dot(vt, powers.astype(bf16)) * (1.0 / total))
                lse[0, head : head + 1, span] = top + jnp.log(total)
            outs.append(jnp.concatenate(parts, axis=1))
        mixed[:, lanes] = jnp.concatenate(outs, axis=0).T.astype(bf16)
    acc_s[...] += dot(mixed[...], wout[0])

    @pl.when(step == pl.num_programs(0) - 1)
    def _():
        mid = x_s[...] + acc_s[...]
        middle[...] = mid
        nf = (mid * rms_factor(mid) * gain_ffn[layer : layer + 1, :]).astype(bf16)
        spread = dot(nf, jnp.concatenate(pieces_of(router[0]), axis=1))
        logits = (
            spread[:, 2 * experts :] + spread[:, experts : 2 * experts] + spread[:, :experts]
        )
        powers = jnp.exp(logits - jnp.max(logits, axis=-1, keepdims=True))
        prob[...] = powers / jnp.sum(powers, axis=-1, keepdims=True)
        cut(dot(place_matrix(rowid_row[0], experts * buffer[0].shape[0]), nf), buffer)


def whole(array):
    zeros = (0,) * array.ndim
    return pl.BlockSpec(array.shape, lambda g: zeros)


def whole_shape(shape):
    zeros = (0,) * len(shape)
    return pl.BlockSpec(shape, lambda g: zeros)


def of_layer(array, layer):
    place = (layer,) + (0,) * (array.ndim - 1)
    return pl.BlockSpec((1,) + array.shape[1:], lambda g: place)


def qkv_specs(width, layer):
    per = width // GROUP
    return [
        pl.BlockSpec(
            (1, width, GROUP), functools.partial(lambda part, g: (layer, 0, part * per + g), part)
        )
        for part in range(3)
    ]


def group_specs(width, layer):
    return (
        pl.BlockSpec((1, GROUP, width), lambda g: (layer, g, 0)),
        pl.BlockSpec((1, GROUP_HEADS, WINDOW_ROWS, SPAN), lambda g: (layer, g, 0, 0)),
    )


def attend(layer, source, common):
    qkv_w, router = common["qkv_w"], common["router"]
    width = qkv_w.shape[1]
    groups = width // GROUP
    experts = router.shape[2]
    out_spec, window_spec = group_specs(width, layer)
    ins, specs = [], []

    def add(array, spec=None):
        ins.append(array)
        specs.append(whole(array) if spec is None else spec)

    if layer > 0:
        add(source["middle"])
        add(source["prob"])
        for name in ("rowcol", "route"):
            add(common[name], of_layer(common[name], layer - 1))
        for block in source["back"]:
            add(block)
    else:
        add(source)
    add(common["gain_attn"])
    for spec in qkv_specs(width, layer):
        add(qkv_w, spec)
    add(common["out_w"], out_spec)
    add(common["windows"], window_spec)
    add(common["seg_row"])
    add(common["seg_col"])
    add(common["gain_ffn"])
    add(router, of_layer(router, layer))
    add(common["rowrow"], of_layer(common["rowrow"], layer))
    block = (common["capacity"], width)
    shapes = [
        ((3, LEN, width), bf16, pl.BlockSpec((3, LEN, GROUP), lambda g: (0, 0, g))),
        ((LEN, width), bf16, pl.BlockSpec((LEN, GROUP), lambda g: (0, g))),
        ((groups, 8, LEN), f32, pl.BlockSpec((1, 8, LEN), lambda g: (g, 0, 0))),
        ((LEN, width), f32, whole_shape((LEN, width))),
        ((LEN, experts), f32, whole_shape((LEN, experts))),
    ] + [(block, bf16, whole_shape(block))] * experts
    if layer > 0:
        shapes = [((LEN, width), f32, whole_shape((LEN, width)))] + shapes
    return pl.pallas_call(
        lambda *refs: attend_kernel(layer, experts, refs),
        grid=(groups,),
        in_specs=specs,
        out_specs=[s[2] for s in shapes],
        out_shape=[jax.ShapeDtypeStruct(s[0], s[1]) for s in shapes],
        scratch_shapes=[
            pltpu.VMEM((LEN, width), bf16),
            pltpu.VMEM((LEN, width), f32),
            pltpu.VMEM((LEN, width), f32),
            pltpu.VMEM((LEN, LEN), f32),
        ],
        compiler_params=params(),
        cost_estimate=QUICK,
        name="attend",
    )(*ins)


def attend_back_kernel(layer, experts, refs):
    refs = list(refs)
    take = lambda count: [refs.pop(0) for _ in range(count)]
    first_layer = layer == 0
    gradient, rowcol, gate_grad, prob, route_col, middle, gain_ffn, router = take(8)
    gback = take(experts)
    x_ref, gain_attn, wq, wk, wv, wout, proj, mixed, lse, windows, seg_row, seg_col, onehot = take(13)
    if not first_layer:
        rowrow_prev, rowcol_prev, prob_prev, route_prev = take(4)
        back_prev = take(experts)
    grad_in, big = take(2)
    if not first_layer:
        (gate_grad_prev,) = take(1)
        buffer_prev = take(experts)
    normt_s, mg_s, att_s, acc_s, mask_s, small_s, rel_s = take(7)
    step = pl.program_id(0)
    width = att_s.shape[1]
    places = dict(
        q=0, k=width, small=2 * width, v=2 * width + SMALL_ROWS, out=3 * width + SMALL_ROWS
    )
    columns = pl.ds(pl.multiple_of(step * GROUP, GROUP), GROUP)

    @pl.when(step == 0)
    def _():
        g = gradient[...].astype(f32)
        rows = join(gback)
        expert_part = dot(take_matrix(rowcol[0], rows.shape[0]), rows)
        probability = prob[...]
        chosen = route_onehot(route_col[0], experts)
        gate = jnp.sum(probability * chosen, axis=-1, keepdims=True)
        logit_grad = gate_grad[...] * gate * (chosen - probability)
        mid = middle[...]
        r = rms_factor(mid)
        scaled = mid * r
        gain = gain_ffn[layer : layer + 1, :]
        nf = (scaled * gain).astype(bf16)
        small_s[...] = jnp.zeros_like(small_s)
        l1, l2, l3 = pieces_of(logit_grad)
        w1, w2, w3 = pieces_of(router[0])
        spread = dot(jnp.concatenate([l1, l2, l3], axis=1), nf, TN)
        small_s[:experts] = (
            spread[2 * experts :] + spread[experts : 2 * experts] + spread[:experts]
        )
        ffn_in = expert_part + dot(
            jnp.concatenate([l1, l1, l2, l2, l1, l3], axis=1),
            jnp.concatenate([w1, w2, w1, w2, w3, w1], axis=1),
            NT,
        )
        u = ffn_in * gain
        mg = g + r * (u - scaled * (r * jnp.mean(u * mid, axis=-1, keepdims=True)))
        small_s[experts + 1 : experts + 2] = jnp.sum(ffn_in * scaled, axis=0, keepdims=True)
        mg_s[...] = mg
        att_s[...] = mg.astype(bf16)
        x = x_ref[...].astype(f32)
        normed = (x * rms_factor(x) * gain_attn[layer : layer + 1, :]).astype(bf16)
        normt_s[...] = normed.T
        acc_s[...] = jnp.zeros_like(acc_s)
        mask_s[...] = mask_of(seg_col[...], seg_row[...])

    att = att_s[...]
    out_rows = pl.ds(pl.multiple_of(places["out"] + step * GROUP, SMALL_ROWS), GROUP)
    big[out_rows, :] = dot(mixed[...], att, TN).astype(big.dtype)
    mixed_grad = dot(att, wout[0], NT).astype(bf16)
    dqs, dks, dvs, rel_rows = [], [], [], []
    for pair in range(GROUP_HEADS // 2):
        lanes = slice(pair * PAIR, (pair + 1) * PAIR)
        q2 = proj[0, :, lanes].astype(f32) * HEAD_DIM ** (-0.5)
        k2 = proj[1, :, lanes]
        v2 = proj[2, :, lanes]
        k2t = k2.T
        o2 = mixed_grad[:, lanes].astype(f32)
        dk = jnp.zeros((LEN, PAIR), f32)
        dv = jnp.zeros((LEN, PAIR), f32)
        dqts = []
        for half in range(2):
            head = pair * 2 + half
            qm = (q2 * half_mask(half)).astype(bf16)
            om = (o2 * half_mask(half)).astype(bf16)
            kt = k2t[half * HEAD_DIM : (half + 1) * HEAD_DIM, :]
            blocks = bias_blocks(windows[0, head])
            sums = {}
            parts = []
            for first in range(0, LEN, QUERY_SPAN):
                span = slice(first, first + QUERY_SPAN)
                scores = dot(k2, qm[span], NT)
                scores = scores + bias_part(blocks, first, QUERY_SPAN) + mask_s[:, span]
                powers = jnp.exp(scores - lse[0, head : head + 1, span])
                prob_grad = dot(v2, om[span], NT)
                weighted = powers * prob_grad
                delta = jnp.sum(weighted, axis=0, keepdims=True)
                score_grad = weighted - powers * delta
                for kb in range(LEN // SIDE):
                    for qb in range(QUERY_SPAN // SIDE):
                        piece = score_grad[kb * SIDE : (kb + 1) * SIDE, qb * SIDE : (qb + 1) * SIDE]
                        offset = offset_of(kb, qb + first // SIDE)
                        sums[offset] = sums[offset] + piece if offset in sums else piece
                sg = score_grad.astype(bf16)
                dv = dv + dot(powers.astype(bf16), om[span])
                dk = dk + dot(sg, qm[span])
                parts.append(dot(kt, sg))
            dqts.append(jnp.concatenate(parts, axis=1))
            rel_rows.append(
                [diagonal_sums(sums[offset]) for offset in (-1, 0, 1)]
                + [
                    jnp.concatenate(
                        [jnp.sum(sums[offset], axis=0, keepdims=True)] + [jnp.zeros((1, SPAN - SIDE), f32)],
                        axis=1,
                    )
                    for offset in (-2, 2)
                ]
            )
        dqs.append((jnp.concatenate(dqts, axis=0) * HEAD_DIM ** (-0.5)).T)
        dks.append(dk)
        dvs.append(dv)
    total = acc_s[...]
    for name, weight, pieces in (("q", wq, dqs), ("k", wk, dks), ("v", wv, dvs)):
        part = jnp.concatenate(pieces, axis=1).astype(bf16)
        first = places[name]
        big[first : first + width, columns] = dot(normt_s[...], part).astype(big.dtype)
        total = total + dot(part, weight[0], NT)
    acc_s[...] = total
    for group in range(width // GROUP):

        @pl.when(step == group)
        def _(group=group):
            for index, rows in enumerate(rel_rows):
                at = group * GROUP_HEADS + index
                for kind, row in enumerate(rows):
                    rel_s[kind, at : at + 1, :] = row

    @pl.when(step == pl.num_programs(0) - 1)
    def _():
        x = x_ref[...].astype(f32)
        r = rms_factor(x)
        scaled = x * r
        attn_in = acc_s[...]
        u = attn_in * gain_attn[layer : layer + 1, :]
        g = mg_s[...] + r * (u - scaled * (r * jnp.mean(u * x, axis=-1, keepdims=True)))
        small_s[experts : experts + 1] = jnp.sum(attn_in * scaled, axis=0, keepdims=True)
        heads = width // HEAD_DIM
        bucket_sums = jnp.zeros((heads, BUCKETS), f32)
        for kind in range(5):
            bucket_sums = bucket_sums + dot(
                rel_s[kind], onehot[kind * SPAN : (kind + 1) * SPAN], precision=highest
            )
        small_s[experts + 2 : experts + 2 + heads, :BUCKETS] = bucket_sums
        big[places["small"] : places["small"] + SMALL_ROWS, :] = small_s[...].astype(big.dtype)
        big[places["out"] + width :, :] = jnp.zeros((SMALL_ROWS, width), big.dtype)
        grad_in[...] = g
        if not first_layer:
            send_back(
                g, back_prev, rowrow_prev, rowcol_prev, prob_prev, route_prev, buffer_prev, gate_grad_prev
            )


def send_back(g, back, rowrow, rowcol, prob, route_col, buffer, gate_grad):
    rows = join(back)
    returned = dot(take_matrix(rowcol[0], rows.shape[0]), rows)
    chosen = route_onehot(route_col[0], prob.shape[1])
    gate = jnp.sum(prob[...] * chosen, axis=-1, keepdims=True)
    gate_grad[...] = jnp.sum(g * returned, axis=-1, keepdims=True)
    expert_grad = (gate * g).astype(bf16)
    cut(dot(place_matrix(rowrow[0], rows.shape[0]), expert_grad), buffer)
    return gate * returned


def attend_back(layer, states, gradient, gback, gate_grad, common):
    state = states[layer]
    qkv_w, router = common["qkv_w"], common["router"]
    width = qkv_w.shape[1]
    groups = width // GROUP
    experts = router.shape[2]
    out_spec, window_spec = group_specs(width, layer)
    ins, specs = [], []

    def add(array, spec=None):
        ins.append(array)
        specs.append(whole(array) if spec is None else spec)

    add(gradient)
    add(common["rowcol"], of_layer(common["rowcol"], layer))
    add(gate_grad)
    add(state["prob"])
    add(common["route"], of_layer(common["route"], layer))
    add(state["middle"])
    add(common["gain_ffn"])
    add(router, of_layer(router, layer))
    for block in gback:
        add(block)
    add(state["x"])
    add(common["gain_attn"])
    for spec in qkv_specs(width, layer):
        add(qkv_w, spec)
    add(common["out_w"], out_spec)
    add(state["proj"], pl.BlockSpec((3, LEN, GROUP), lambda g: (0, 0, g)))
    add(state["mixed"], pl.BlockSpec((LEN, GROUP), lambda g: (0, g)))
    add(state["lse"], pl.BlockSpec((1, 8, LEN), lambda g: (g, 0, 0)))
    add(common["windows"], window_spec)
    add(common["seg_row"])
    add(common["seg_col"])
    add(common["onehot"])
    payload = (4 * width + 2 * SMALL_ROWS, width)
    shapes = [((LEN, width), f32), (payload, bf16)]
    if layer > 0:
        for name in ("rowrow", "rowcol"):
            add(common[name], of_layer(common[name], layer - 1))
        add(states[layer - 1]["prob"])
        add(common["route"], of_layer(common["route"], layer - 1))
        for block in states[layer - 1]["back"]:
            add(block)
        shapes += [((LEN, 1), f32)] + [((common["capacity"], width), bf16)] * experts
    return pl.pallas_call(
        lambda *refs: attend_back_kernel(layer, experts, refs),
        grid=(groups,),
        in_specs=specs,
        out_specs=[whole_shape(s[0]) for s in shapes],
        out_shape=[jax.ShapeDtypeStruct(s[0], s[1]) for s in shapes],
        scratch_shapes=[
            pltpu.VMEM((width, LEN), bf16),
            pltpu.VMEM((LEN, width), f32),
            pltpu.VMEM((LEN, width), bf16),
            pltpu.VMEM((LEN, width), f32),
            pltpu.VMEM((LEN, LEN), f32),
            pltpu.VMEM((SMALL_ROWS, width), f32),
            pltpu.VMEM((5, width // HEAD_DIM, SPAN), f32),
        ],
        compiler_params=params(),
        cost_estimate=QUICK,
        name="attend_back",
    )(*ins)


def turn_kernel(experts, refs):
    middle, cotangent, rowrow, rowcol, prob, route_col = refs[:6]
    back = refs[6 : 6 + experts]
    output, gate_grad = refs[6 + experts : 8 + experts]
    buffer = refs[8 + experts :]
    g = cotangent[...].astype(f32)
    added = send_back(g, back, rowrow, rowcol, prob, route_col, buffer, gate_grad)
    output[...] = middle[...] + added


def turn(layer, state, cotangent, common):
    width = cotangent.shape[1]
    experts = len(state["back"])
    ins = [state["middle"], cotangent, common["rowrow"], common["rowcol"], state["prob"]]
    ins += [common["route"]] + list(state["back"])
    specs = [whole(array) for array in ins]
    for index in (2, 3, 5):
        specs[index] = of_layer(ins[index], layer)
    shapes = [((LEN, width), f32), ((LEN, 1), f32)]
    shapes += [((common["capacity"], width), bf16)] * experts
    return pl.pallas_call(
        lambda *refs: turn_kernel(experts, refs),
        grid=(1,),
        in_specs=specs,
        out_specs=[whole_shape(s[0]) for s in shapes],
        out_shape=[jax.ShapeDtypeStruct(s[0], s[1]) for s in shapes],
        compiler_params=params(),
        cost_estimate=QUICK,
        name="turn",
    )(*ins)


GELU_A = float(np.sqrt(2.0 / np.pi))
GELU_B = 0.044715


def gelu_tanh(hidden):
    return jnp.tanh(GELU_A * (hidden + GELU_B * (hidden * hidden * hidden)))


def gelu_of(hidden, curve):
    return 0.5 * hidden * (1.0 + curve)


def gelu_slope(hidden, curve):
    inner = GELU_A * (1.0 + (3.0 * GELU_B) * (hidden * hidden))
    return 0.5 * (1.0 + curve) + 0.5 * hidden * (1.0 - curve * curve) * inner


def expert_kernel(experts, refs):
    blocks = refs[:experts]
    w_in, w_out, rows = refs[experts : experts + 3]
    outs = refs[experts + 3 : -1]
    acc = refs[-1]
    step = pl.program_id(0)

    @pl.when(step == 0)
    def _():
        rows[...] = join(blocks)
        acc[...] = jnp.zeros_like(acc)

    hidden = dot(rows[...], w_in[...])
    active = gelu_of(hidden, gelu_tanh(hidden)).astype(bf16)
    acc[...] += dot(active, w_out[...])

    @pl.when(step == pl.num_programs(0) - 1)
    def _():
        cut(acc[...], outs)


def weight_specs(weights):
    if len(weights) == 1:
        width = weights[0].shape[1]
        return [
            pl.BlockSpec((width, width), lambda b: (2 * b, 0)),
            pl.BlockSpec((width, width), lambda b: (2 * b + 1, 0)),
        ]
    parts = weights[0].shape[0] // weights[1].shape[1]
    return [
        pl.BlockSpec((array.shape[0] // parts, array.shape[1]), lambda b: (b, 0))
        for array in weights
    ]


def expert(blocks, weights, parts):
    experts = len(blocks)
    capacity, width = blocks[0].shape
    count = experts * capacity
    rows_shape = jax.ShapeDtypeStruct((count, width), bf16)
    specs = [whole(block) for block in blocks]
    hidden = weights[-1].shape[0] // (2 if len(weights) == 1 else 1)
    results = pl.pallas_call(
        lambda *refs: expert_kernel(experts, refs),
        grid=(parts,),
        in_specs=specs + weight_specs(weights),
        out_specs=[whole_shape((count, width))] + specs,
        out_shape=[rows_shape] + [jax.ShapeDtypeStruct(b.shape, bf16) for b in blocks],
        scratch_shapes=[pltpu.VMEM((count, width), f32)],
        compiler_params=params(),
        cost_estimate=QUICK,
        name="expert",
    )(*blocks, *(weights * 2)[:2])
    return results[0], results[1:]


def expert_back_kernel(experts, refs):
    rows = refs[0]
    blocks = refs[1 : 1 + experts]
    w_in, w_out, grads = refs[1 + experts : 4 + experts]
    outs = refs[4 + experts : -1]
    acc = refs[-1]
    step = pl.program_id(0)

    @pl.when(step == 0)
    def _():
        grads[...] = join(blocks)
        acc[...] = jnp.zeros_like(acc)

    hidden = dot(rows[...], w_in[...])
    act_grad = dot(grads[...], w_out[...], NT)
    pre_grad = (act_grad * gelu_slope(hidden, gelu_tanh(hidden))).astype(bf16)
    acc[...] += dot(pre_grad, w_in[...], NT)

    @pl.when(step == pl.num_programs(0) - 1)
    def _():
        cut(acc[...], outs)


def expert_back(rows, blocks, weights, parts):
    experts = len(blocks)
    count, width = rows.shape
    specs = [whole(block) for block in blocks]
    hidden = weights[-1].shape[0] // (2 if len(weights) == 1 else 1)
    results = pl.pallas_call(
        lambda *refs: expert_back_kernel(experts, refs),
        grid=(parts,),
        in_specs=[whole(rows)] + specs + weight_specs(weights),
        out_specs=[whole(rows)] + specs,
        out_shape=[jax.ShapeDtypeStruct(a.shape, bf16) for a in [rows] + list(blocks)],
        scratch_shapes=[pltpu.VMEM((count, width), f32)],
        compiler_params=params(),
        cost_estimate=QUICK,
        name="expert_back",
    )(rows, *blocks, *(weights * 2)[:2])
    return results[0], results[1:]


def weight_grad_kernel(order, rows, grads, w_in, w_out, *refs):
    g_in, g_out = refs[-2:]
    step = pl.program_id(0)

    @pl.when(step == 0)
    def _():
        g_in[...] = jnp.zeros_like(g_in)
        g_out[...] = jnp.zeros_like(g_out)

    hidden = dot(rows[...], w_in[0, 0])
    curve = gelu_tanh(hidden)
    active = gelu_of(hidden, curve).astype(bf16)
    act_grad = dot(grads[...], w_out[0, 0], NT)
    pre_grad = (act_grad * gelu_slope(hidden, curve)).astype(bf16)
    g_out[0, 0] += dot(active, grads[...], TN)
    g_in[0, 0] += dot(rows[...], pre_grad, TN)


def weight_grad(layer, order, rows_all, grads_all, w_in, w_out, into):
    width = w_in.shape[2]
    parts = order.shape[0]
    count = rows_all.shape[0] // parts

    def part_of(array):
        return pl.BlockSpec((1, 1) + array.shape[2:], lambda b, order: (layer, 0, 0, 0))

    specs = [part_of(w_in), part_of(w_out)]
    grid_spec = pltpu.PrefetchScalarGridSpec(
        num_scalar_prefetch=1,
        grid=(parts,),
        in_specs=[
            pl.BlockSpec((count, width), lambda b, order: (order[b], 0)),
            pl.BlockSpec((count, width), lambda b, order: (b, 0)),
        ]
        + specs
        + [pl.BlockSpec(memory_space=pl.ANY)] * len(into),
        out_specs=specs,
    )
    return pl.pallas_call(
        weight_grad_kernel,
        grid_spec=grid_spec,
        out_shape=[
            jax.ShapeDtypeStruct(w_in.shape, f32),
            jax.ShapeDtypeStruct(w_out.shape, f32),
        ],
        input_output_aliases={5 + index: index for index in range(len(into))},
        compiler_params=params(),
        cost_estimate=QUICK,
        name="weight_grad",
    )(order, rows_all, grads_all, w_in, w_out, *into)


def finish_kernel(side, first, second, qkv, out):
    kind = pl.program_id(0) % 4
    upper = (side[0] + jnp.where(kind >= 2, 1, 0)) % 2
    values = jnp.where(upper == 0, first[...].astype(f32), second[...].astype(f32))

    @pl.when(kind < 3)
    def _():
        qkv[0] = values

    @pl.when(kind == 3)
    def _():
        out[0] = values


def finish(side, first, second):
    width = first.shape[1] // LAYERS

    def rows_of(turned):
        def place(step, side):
            kind = step % 4
            lower, higher = jnp.minimum(kind, 1), jnp.maximum(kind, 2) - 2
            return jnp.where(side[0] == turned, lower, higher), step // 4

        return pl.BlockSpec((width, width), place)

    grid_spec = pltpu.PrefetchScalarGridSpec(
        num_scalar_prefetch=1,
        grid=(4 * LAYERS,),
        in_specs=[rows_of(0), rows_of(1)],
        out_specs=[
            pl.BlockSpec(
                (1, width, width), lambda step, side: (step // 4, 0, jnp.minimum(step % 4, 2))
            ),
            pl.BlockSpec((1, width, width), lambda step, side: (step // 4, 0, 0)),
        ],
    )
    return pl.pallas_call(
        finish_kernel,
        grid_spec=grid_spec,
        out_shape=[
            jax.ShapeDtypeStruct((LAYERS, width, 3 * width), f32),
            jax.ShapeDtypeStruct((LAYERS, width, width), f32),
        ],
        compiler_params=params(),
        cost_estimate=QUICK,
        name="finish",
    )(side.reshape(1), first, second)


def partner(array, axis, bit):
    pairs = [(index, index ^ bit) for index in range(lax.axis_size(axis))]
    return lax.ppermute(array, axis, pairs)


def swap(blocks):
    return [blocks[0]] + [partner(block, "dp", k) for k, block in enumerate(blocks) if k > 0]


def gather_rows(rows):
    return lax.all_gather(rows, "mp", axis=0, tiled=True)


def gather_weights(w_in, w_out, layer):
    first, second = w_in[layer, 0], w_out[layer, 0]
    if first.shape == second.shape:
        joined = jnp.concatenate([first, second], axis=0)
        return (lax.all_gather(joined, "mp", axis=0, tiled=True),)
    return tuple(lax.all_gather(part, "mp", axis=0, tiled=True) for part in (first, second))


def bit_of(step):
    axis, bit = step
    return (lax.axis_index(axis) // bit) % 2


def add_rounded(kept, received):
    return (kept.astype(f32) + received.astype(f32)).astype(kept.dtype)


def halve(array, step):
    half = array.shape[0] // 2
    mine = bit_of(step)
    kept = lax.dynamic_slice_in_dim(array, mine * half, half, 0)
    sent = lax.dynamic_slice_in_dim(array, (1 - mine) * half, half, 0)
    return kept, sent


def bits_of(axis):
    size = lax.axis_size(axis)
    return [(axis, 1 << place) for place in range(size.bit_length() - 1)]


def sum_of_cores(payload):
    core = bits_of("dp")[0]
    kept, sent = halve(payload, core)
    return add_rounded(kept, partner(sent, *core))


def sum_everywhere(total, beside):
    along_dp, along_mp = bits_of("dp"), bits_of("mp")
    core, along_z = along_dp[0], along_dp[1:]
    half_mp = len(along_mp) // 2
    inner, outer = along_mp[:half_mp], along_mp[half_mp:]
    near, far = along_z[:1], along_z[1:]
    orders = [inner + outer + near + far, outer + near + inner + far, near + inner + outer + far]
    unit = 1 << len(orders[0])
    units = total.shape[0] // unit
    sizes = [(units + 2 - index) // 3 * unit for index in range(3)]
    starts = [0, sizes[0], sizes[0] + sizes[1]]
    parts = [total[start : start + size] for start, size in zip(starts, sizes)]
    for level in range(len(orders[0])):
        steps = [order[level] for order in orders]
        halves = [halve(part, step) for part, step in zip(parts, steps)]
        received = [partner(half[1], *step) for half, step in zip(halves, steps)]
        received = lax.optimization_barrier(received)
        if level == 0:
            received, beside = lax.optimization_barrier((received, beside))
        parts = [add_rounded(half[0], other) for half, other in zip(halves, received)]
        parts = lax.optimization_barrier(parts)
    for level in reversed(range(len(orders[0]))):
        steps = [order[level] for order in orders]
        received = [partner(part, *step) for part, step in zip(parts, steps)]
        received = lax.optimization_barrier(received)
        parts = [
            jnp.where(
                bit_of(step) == 0,
                jnp.concatenate([part, other], axis=0),
                jnp.concatenate([other, part], axis=0),
            )
            for part, other, step in zip(parts, received, steps)
        ]
    mine = jnp.concatenate(parts, axis=0)
    return mine, partner(mine, *core), beside


def body(
    tokens,
    segments,
    routes,
    gain_attn,
    qkv_weight,
    out_weight,
    rel_bias,
    gain_ffn,
    router_weight,
    w_in,
    w_out,
    cotangent,
):
    tok_count, width = tokens.shape
    experts = w_in.shape[1] * lax.axis_size("dp")
    parts = lax.axis_size("mp")
    capacity = (tok_count * 9 + 8 * experts - 1) // (8 * experts)
    heads = width // HEAD_DIM

    weights = [gather_weights(w_in, w_out, layer) for layer in range(LAYERS)]
    onehot = window_onehot()
    windows = jnp.einsum("pb,lbh->lhp", onehot, rel_bias, precision=highest)
    chosen = routes[:, :, 0]
    chosen_onehot = (
        chosen[:, :, None] == jnp.arange(experts, dtype=jnp.int32)[None, None, :]
    ).astype(jnp.int32)
    slots = jnp.sum(jnp.cumsum(chosen_onehot, axis=1) * chosen_onehot, axis=-1) - 1
    rowid = (chosen ^ lax.axis_index("dp")) * capacity + slots
    common = dict(
        gain_attn=gain_attn,
        gain_ffn=gain_ffn,
        qkv_w=qkv_weight,
        out_w=out_weight,
        router=router_weight,
        windows=windows.reshape(LAYERS, heads, WINDOW_ROWS, SPAN),
        onehot=onehot,
        seg_row=segments.reshape(1, LEN),
        seg_col=segments.reshape(LEN, 1),
        rowrow=rowid[:, None, :],
        rowcol=rowid[:, :, None],
        route=routes,
        capacity=capacity,
    )

    states = []
    source = tokens
    for layer in range(LAYERS):
        results = list(attend(layer, source, common))
        state = dict(x=results.pop(0) if layer > 0 else tokens)
        for name in ("proj", "mixed", "lse", "middle", "prob"):
            state[name] = results.pop(0)
        state["rows"], outs = expert(swap(results), weights[layer], parts)
        state["back"] = swap(outs)
        states.append(state)
        source = state

    rows_all = [gather_rows(state["rows"]) for state in states]
    output, gate_grad, *blocks = turn(LAYERS - 1, states[-1], cotangent, common)
    gradient = cotangent
    totals = [None] * LAYERS
    held = []
    order = jnp.arange(parts, dtype=jnp.int32)
    weight_grads = ()
    for layer in reversed(range(LAYERS)):
        last = layer == 0
        arrived = swap(blocks)
        if layer == LAYERS - 1:
            arrived, rows_all[0] = lax.optimization_barrier((arrived, rows_all[0]))
        else:
            arrived, weight_grads = lax.optimization_barrier((arrived, weight_grads))
        grads, sent = expert_back(states[layer]["rows"], arrived, weights[layer], parts)
        gback = swap(sent)
        if layer > 0:
            gback, rows_all[layer] = lax.optimization_barrier((gback, rows_all[layer]))
        else:
            gback[1], held = lax.optimization_barrier((gback[1], held))
            totals[1:] = [sum_of_cores(array) for array in held]
            gback, totals[1:] = lax.optimization_barrier((gback, totals[1:]))
        grads_all = gather_rows(grads)
        results = attend_back(layer, states, gradient, gback, gate_grad, common)
        gradient, payload = results[:2]
        if layer > 0:
            gate_grad, *blocks = results[2:]
            held.insert(0, payload)
        else:
            payload, grads_all = lax.optimization_barrier((payload, grads_all))
            totals[layer] = sum_of_cores(payload)
            totals[layer], grads_all = lax.optimization_barrier((totals[layer], grads_all))
        weight_grads = weight_grad(
            layer, order, rows_all[layer], grads_all, w_in, w_out, tuple(weight_grads)
        )
    total = jnp.concatenate(totals, axis=1)
    mine, other, (grad_w_in, grad_w_out) = sum_everywhere(total, weight_grads)
    side = lax.axis_index("dp").astype(jnp.int32) % 2
    grad_qkv, grad_out = finish(side, mine, other)
    rows = jnp.where(side == 0, mine[2 * width :], other[2 * width :]).astype(f32)
    small = [rows[:, layer * width : (layer + 1) * width] for layer in range(LAYERS)]
    grad_gain_attn = jnp.stack([rows[experts] for rows in small])
    grad_gain_ffn = jnp.stack([rows[experts + 1] for rows in small])
    grad_router = jnp.stack([rows[:experts].T for rows in small])
    grad_rel = jnp.stack([rows[experts + 2 : experts + 2 + heads, :BUCKETS].T for rows in small])
    return (
        output,
        gradient,
        grad_gain_attn,
        grad_qkv,
        grad_out,
        grad_rel,
        grad_gain_ffn,
        grad_router,
        grad_w_in,
        grad_w_out,
    )


def solution(mesh):
    return jax.shard_map(
        body,
        mesh=mesh,
        in_specs=(
            P(("dp", "mp"), None),
            P(("dp", "mp"), None),
            P(None, ("dp", "mp"), None),
            P(),
            P(),
            P(),
            P(),
            P(),
            P(),
            P(None, "dp", None, "mp"),
            P(None, "dp", "mp", None),
            P(("dp", "mp"), None),
        ),
        out_specs=(
            P(("dp", "mp"), None),
            P(("dp", "mp"), None),
            P(),
            P(),
            P(),
            P(),
            P(),
            P(),
            P(None, "dp", None, "mp"),
            P(None, "dp", "mp", None),
        ),
        check_vma=False,
    )
```
